32 devices in a mesh: ens: 2 (over y), seq: 4 (over z), mp: 2 (over x), sub: 2 (over core).
Axes of the slice: x: 2, y: 2, z: 4, core: 2. Of those that a mesh axis runs over, the one named last changes fastest.
Arguments:
- grid_latent: bfloat16 [16384, 1024], P(('ens', 'seq'), ('mp', 'sub')), parts along dimension 0, may hold values from -6 to 6
- grid_count: int32 [8], P(('ens', 'seq')), parts along dimension 0, may hold values from 1024 to 2048, as said below
- hidden_embed: bfloat16 [8192, 1024], P(('ens', 'seq'), ('mp', 'sub')), parts along dimension 0, may hold values from -6 to 6
- enc_src_rows: int32 [8, 32, 128], P(('ens', 'seq')), parts along dimension 0, may hold values from 0 to 2047, as said below
- enc_dst_rows: int32 [8, 32, 128], P(('ens', 'seq')), parts along dimension 0, may hold values from 0 to 1023
- enc_weight: float32 [8, 32, 128], P(('ens', 'seq')), parts along dimension 0, may hold values from 0.25 to 1
- dec_src_rows: int32 [8, 48, 128], P(('ens', 'seq')), parts along dimension 0, may hold values from 0 to 1023
- dec_dst_rows: int32 [8, 48, 128], P(('ens', 'seq')), parts along dimension 0, may hold values from 0 to 2047, as said below
- dec_weight: float32 [8, 48, 128], P(('ens', 'seq')), parts along dimension 0, may hold values from 0.25 to 1
- norm_gain: float32 [1024], replicated, may hold values from 0.1 to 1.9
- w_qkv: bfloat16 [1024, 3072], P(None, ('mp', 'sub'))
- w_out: bfloat16 [1024, 1024], P(('mp', 'sub')), may hold values from -0.1875 to 0.1875
- w_up: bfloat16 [1024, 4096], P(None, ('mp', 'sub')), may hold values from -0.1875 to 0.1875
- up_exp: int32 [4096], P(('mp', 'sub')), may hold values from -1 to 1
- w_down: bfloat16 [4096, 1024], P(('mp', 'sub')), may hold values from -0.09375 to 0.09375
- down_exp: int32 [1024], replicated, may hold values from -1 to 1
Outputs:
- hidden_out: bfloat16 [8192, 1024], P(('ens', 'seq'), ('mp', 'sub')), parts along dimension 0
- grid_out: bfloat16 [16384, 1024], P(('ens', 'seq'), ('mp', 'sub')), parts along dimension 0
The draws below stay inside these ranges and needn't reach their ends.
There are 2 independent parts, one for each index of `ens`. The reference program is written for one: setup_inputs(seed, part) draws one part's arguments, and reference() takes and returns one part's arrays. A program takes and returns all parts, laid end to end along the dimension named above; an argument that names none is the same for every part. Nothing has to cross between parts.
Inputs may be any that keep to these rules, and one draw needn't show every extreme that they name: `grid_count`: each block holds between 1024 and 2048 live grid nodes; some block holds exactly 2048. `enc_src_rows`: each source row is below grid_count of its sending block s. `dec_dst_rows`: each destination row is below grid_count of its receiving block d.
All inputs are finite; a program needn't handle non-finite values.
Results may differ from the reference program's by a relative error of at most 0.013.
Values may be sent and summed in bfloat16 or wider, within the bound.
A program may use at most 128 MiB of HBM per device.

```python
import math
import jax
import jax.numpy as jnp
from jax import lax

D = 1024
HEADS = 16
HD = 64
FFW = 4096
WIN = 512
TILE = 128
ESIDE = 4
ELOCAL = 24
DSIDE = 4
DLOCAL = 40
HID_DEV = 1024
GCAP = 2048
ETILES = 32
DTILES = 48
HID_TOTAL = 4096
GRID = 8192
N_SEQ = 4
N_MP = 2
N_SUB = 2


def owner_counts(key):
    counts = jax.random.randint(jax.random.fold_in(key, 101), (N_SEQ,), GCAP // 2, GCAP + 1)
    full_owner = jax.random.randint(jax.random.fold_in(key, 102), (), 0, N_SEQ)
    return jnp.where(jnp.arange(N_SEQ) == full_owner, GCAP, counts).astype(jnp.int32)


def draw_grid_count(key, part):
    return owner_counts(key)


def draw_enc_src_rows(key, part):
    limits = owner_counts(key)[:, None, None]
    return jax.random.randint(jax.random.fold_in(key, 103), (N_SEQ, ELOCAL + 2 * ESIDE, TILE), 0, limits).astype(jnp.int32)


def draw_dec_dst_rows(key, part):
    limits = owner_counts(key)[:, None, None]
    return jax.random.randint(jax.random.fold_in(key, 104), (N_SEQ, DLOCAL + 2 * DSIDE, TILE), 0, limits).astype(jnp.int32)


def draw_w_qkv(key, part):
    base = jax.random.normal(jax.random.fold_in(key, 111), (D, HEADS, 3, HD), jnp.float32) * D ** (-0.5)
    return base.reshape(D, 3 * D).astype(jnp.bfloat16)


def touch_ends(array, key, low, largest):
    longest = array.shape.index(max(array.shape))
    spots = []
    for shift in (0, 1):
        where = [jax.random.randint(jax.random.fold_in(key, axis), (), 0, length) for axis, length in enumerate(array.shape)]
        where[longest] = (where[longest] + shift) % array.shape[longest]
        spots.append(tuple(where))
    return array.at[spots[0]].set(low).at[spots[1]].set(largest)


def block_scale(stream_key, shape, cuts, low, top_value):
    factor_of, own = 1.0, jax.random.fold_in(stream_key, 6)
    for axis_at, parts in cuts:
        draws = jnp.exp(jax.random.uniform(jax.random.fold_in(own, axis_at), (parts,), jnp.float32, low / len(cuts), top_value / len(cuts)))
        factor_of = factor_of * jnp.repeat(draws, shape[axis_at] // parts).reshape([-1 if axis == axis_at else 1 for axis in range(len(shape))])
    return factor_of


def noise(rng, shape, spread, bound, cuts=(), kind=jnp.bfloat16):
    entries = spread * jax.random.normal(rng, shape, jnp.float32)
    if cuts:
        entries = entries * block_scale(rng, shape, cuts, -0.22, 0.18)
    return jnp.clip(entries, -bound, bound).astype(kind)


def setup_inputs(seed: int = 0, part: int = 0) -> dict:
    key_list = jax.random.split(jax.random.key(seed), 17)
    part_splits = jax.random.split(jax.random.fold_in(key_list[16], part), 17)
    return {
        "grid_latent": noise(part_splits[0], (GRID, D), 1.0, 6.0, ((0, 4), (1, 4))),
        "grid_count": draw_grid_count(jax.random.fold_in(jax.random.fold_in(key_list[16], part), 71), part),
        "hidden_embed": noise(part_splits[2], (HID_TOTAL, D), 1.0, 6.0, ((0, 4), (1, 4))),
        "enc_src_rows": draw_enc_src_rows(jax.random.fold_in(jax.random.fold_in(key_list[16], part), 71), part),
        "enc_dst_rows": touch_ends(jax.random.randint(part_splits[4], (N_SEQ, ETILES, TILE), 0, HID_DEV), jax.random.fold_in(part_splits[4], 1), 0, HID_DEV - 1).astype(jnp.int32),
        "enc_weight": jnp.clip(jnp.exp(math.log(1.0) - 1.3862944 * jax.random.uniform(part_splits[5], (N_SEQ, ETILES, TILE), jnp.float32) ** block_scale(part_splits[5], (N_SEQ, ETILES, TILE), ((0, 4),), -0.2, 0.2)), 0.25, 1.0),
        "dec_src_rows": touch_ends(jax.random.randint(part_splits[6], (N_SEQ, DTILES, TILE), 0, HID_DEV), jax.random.fold_in(part_splits[6], 1), 0, HID_DEV - 1).astype(jnp.int32),
        "dec_dst_rows": draw_dec_dst_rows(jax.random.fold_in(jax.random.fold_in(key_list[16], part), 71), part),
        "dec_weight": jnp.clip(jnp.exp(math.log(1.0) - 1.3862944 * jax.random.uniform(part_splits[8], (N_SEQ, DTILES, TILE), jnp.float32) ** block_scale(part_splits[8], (N_SEQ, DTILES, TILE), ((0, 4),), -0.2, 0.2)), 0.25, 1.0),
        "norm_gain": jnp.clip(1.0 + 0.18 * jax.random.normal(key_list[9], (D,), jnp.float32), 0.1, 1.9),
        "w_qkv": draw_w_qkv(jax.random.fold_in(key_list[16], 71), part),
        "w_out": noise(key_list[11], (D, D), D ** -0.5, 0.1875, ((0, 4),)),
        "w_up": noise(key_list[12], (D, FFW), D ** -0.5, 0.1875, ((1, 4),)),
        "up_exp": touch_ends(jax.random.randint(key_list[13], (FFW,), -1, 2), jax.random.fold_in(key_list[13], 1), -1, 1).astype(jnp.int32),
        "w_down": noise(key_list[14], (FFW, D), FFW ** -0.5, 0.09375, ((0, 4),)),
        "down_exp": touch_ends(jax.random.randint(key_list[15], (D,), -1, 2), jax.random.fold_in(key_list[15], 1), -1, 1).astype(jnp.int32),
    }


def to_half(values):
    return lax.optimization_barrier(values.astype(jnp.bfloat16))

def norm_rows(rows, norm_gain):
    values = rows.astype(jnp.float32)
    row_mean = lax.optimization_barrier(jnp.mean(values, axis=-1, keepdims=True))
    centered = values - row_mean
    row_var = lax.optimization_barrier(jnp.mean(centered * centered, axis=-1, keepdims=True))
    return to_half(centered * lax.rsqrt(row_var + 1e-05) * norm_gain.astype(jnp.float32)[None, :])

def edge_sum(source, src_rows, dst_rows, weights, src_block, dst_block, side):
    blocks = N_SEQ
    width = side * TILE
    block_ids = jnp.arange(blocks, dtype=jnp.int32)
    src = src_rows.reshape(blocks, -1) + (block_ids * src_block)[:, None]
    wts = weights.reshape(blocks, -1)
    dst = dst_rows.reshape(blocks, -1) + (block_ids * dst_block)[:, None]
    left_src = jnp.roll(src[:, width:2 * width], 1, axis=0)
    left_wts = jnp.where((block_ids > 0)[:, None], jnp.roll(wts[:, width:2 * width], 1, axis=0), 0.0)
    right_src = jnp.roll(src[:, :width], -1, axis=0)
    right_wts = jnp.where((block_ids < blocks - 1)[:, None], jnp.roll(wts[:, :width], -1, axis=0), 0.0)
    arr_src = jnp.concatenate([left_src, right_src, src[:, 2 * width:]], axis=1).astype(jnp.int32)
    arr_wts = jnp.concatenate([left_wts, right_wts, wts[:, 2 * width:]], axis=1)

    def add_block(total, pieces):
        src_part, dst_part, weight_part = pieces
        picked = jnp.take(source, src_part, axis=0).astype(jnp.float32) * weight_part[:, None]
        return (total.at[dst_part].add(to_half(picked).astype(jnp.float32)), None)
    start = jnp.zeros((dst_block * blocks, source.shape[1]), jnp.float32)
    total, _ = lax.scan(add_block, start, (arr_src, dst, arr_wts))
    return total

def reference(grid_latent, grid_count, hidden_embed, enc_src_rows, enc_dst_rows, enc_weight, dec_src_rows, dec_dst_rows, dec_weight, norm_gain, w_qkv, w_out, w_up, up_exp, w_down, down_exp):
    blocks = N_SEQ
    hidden_total = HID_DEV * blocks
    encoded = edge_sum(grid_latent, enc_src_rows, enc_dst_rows, enc_weight, GCAP, HID_DEV, ESIDE)
    latent = to_half(hidden_embed.astype(jnp.float32) + encoded)
    normed = norm_rows(latent, norm_gain)
    qkv = jnp.dot(normed, w_qkv, preferred_element_type=jnp.float32).reshape(hidden_total, HEADS, 3, HD)
    queries = to_half(qkv[:, :, 0, :])
    keys = to_half(qkv[:, :, 1, :])
    values = to_half(qkv[:, :, 2, :])
    padding = jnp.zeros((WIN, HEADS, HD), jnp.bfloat16)
    keys_pad = jnp.concatenate([padding, keys, padding], axis=0)
    values_pad = jnp.concatenate([padding, values, padding], axis=0)
    query_rows = min(512, HID_DEV)
    span = query_rows + 2 * WIN
    scale = HD ** (-0.5)

    def attend_block(index):
        start = (index * query_rows).astype(jnp.int32)
        query_block = lax.dynamic_slice_in_dim(queries, start, query_rows, 0).astype(jnp.float32)
        key_block = lax.dynamic_slice_in_dim(keys_pad, start, span, 0).astype(jnp.float32)
        value_block = lax.dynamic_slice_in_dim(values_pad, start, span, 0).astype(jnp.float32)
        scores = jnp.einsum('qhd,khd->hqk', query_block, key_block) * scale
        query_pos = start + jnp.arange(query_rows, dtype=jnp.int32)
        key_pos = start - WIN + jnp.arange(span, dtype=jnp.int32)
        allowed = (jnp.abs(query_pos[:, None] - key_pos[None, :]) <= WIN) & (key_pos[None, :] >= 0) & (key_pos[None, :] < hidden_total)
        scores = jnp.where(allowed[None, :, :], scores, -1e+30)
        peak = lax.optimization_barrier(jnp.max(scores, axis=-1, keepdims=True))
        expo = jnp.exp(scores - peak)
        attn_weights = to_half(expo / lax.optimization_barrier(jnp.sum(expo, axis=-1, keepdims=True))).astype(jnp.float32)
        return to_half(jnp.einsum('hqk,khd->qhd', attn_weights, value_block))
    attended = lax.map(attend_block, jnp.arange(hidden_total // query_rows, dtype=jnp.int32)).reshape(hidden_total, D)
    up_proj = jnp.dot(normed, w_up, preferred_element_type=jnp.float32) * jnp.exp2(up_exp.astype(jnp.float32))[None, :]
    activated = to_half(jax.nn.gelu(up_proj, approximate=False))
    down_scale = jnp.exp2(down_exp.astype(jnp.float32))[None, :]
    shards = N_MP * N_SUB
    head_cols = D // shards
    unit_cols = FFW // shards
    summed = jnp.zeros((hidden_total, D), jnp.float32)
    for shard in range(shards):
        attn_part = jnp.dot(attended[:, shard * head_cols:(shard + 1) * head_cols], w_out[shard * head_cols:(shard + 1) * head_cols], preferred_element_type=jnp.float32)
        mlp_part = jnp.dot(activated[:, shard * unit_cols:(shard + 1) * unit_cols], w_down[shard * unit_cols:(shard + 1) * unit_cols], preferred_element_type=jnp.float32) * down_scale
        summed = summed + to_half(attn_part + mlp_part).astype(jnp.float32)
    hidden_out = to_half(latent.astype(jnp.float32) + summed)
    decoded = edge_sum(hidden_out, dec_src_rows, dec_dst_rows, dec_weight, HID_DEV, GCAP, DSIDE)
    live_rows = (jnp.arange(GCAP, dtype=jnp.int32)[None, :] < grid_count[:, None]).reshape(-1)
    grid_out = jnp.where(live_rows[:, None], grid_latent.astype(jnp.float32) + decoded, 0.0).astype(jnp.bfloat16)
    return (hidden_out.astype(jnp.bfloat16), grid_out)
```

```python
import functools

import jax
import jax.numpy as jnp
from jax import lax
from jax.experimental import pallas as pl
from jax.experimental.pallas import tpu as pltpu
from jax.sharding import PartitionSpec as P

HD = 64
WIN = 512
TILE = 128
ESIDE = 4
DSIDE = 4
GROUP = 8
LIMIT = 56 * 1024 * 1024
VM = pl.BlockSpec(memory_space=pltpu.VMEM)


def params(**more):
    return pltpu.CompilerParams(vmem_limit_bytes=LIMIT, **more)


def turned(row):
    return jnp.broadcast_to(row, (TILE, TILE)).T


def gather_group(src, weight, table):
    rows, columns = table.shape
    lane = lax.broadcasted_iota(jnp.int32, (TILE, rows), 1)
    picks, scales = [], []
    for tile in range(src.shape[0]):
        col = turned(src[tile : tile + 1])
        col = jnp.concatenate([col] * (rows // TILE), axis=1)
        picks.append(jnp.where(lane == col, 1.0, 0.0).astype(jnp.bfloat16))
        scale = turned(weight[tile : tile + 1])
        scales.append(jnp.concatenate([scale] * (columns // TILE), axis=1))
    picked = jnp.dot(jnp.concatenate(picks, axis=0), table, preferred_element_type=jnp.float32)
    return (picked * jnp.concatenate(scales, axis=0)).astype(jnp.bfloat16)


def scatter_group(dst, messages, rows):
    line = lax.broadcasted_iota(jnp.int32, (rows, TILE), 0)
    spots = [
        jnp.where(line == dst[tile : tile + 1], 1.0, 0.0).astype(jnp.bfloat16)
        for tile in range(dst.shape[0])
    ]
    return jnp.dot(jnp.concatenate(spots, axis=1), messages, preferred_element_type=jnp.float32)


def side_kernel(side, src_ref, weight_ref, table_ref, out_ref):
    out_ref[...] = gather_group(src_ref[: 2 * side], weight_ref[: 2 * side], table_ref[...])


def side_messages(source, src_rows, weights, side):
    return pl.pallas_call(
        functools.partial(side_kernel, side),
        out_shape=jax.ShapeDtypeStruct((2 * side * TILE, source.shape[1]), jnp.bfloat16),
        in_specs=[VM] * 3,
        out_specs=VM,
        compiler_params=params(),
        name="side_messages",
    )(src_rows, weights, source)


def local_kernel(side, src_ref, weight_ref, dst_ref, table_ref, out_ref):
    tiles = src_ref.shape[0]
    rows = out_ref.shape[0]
    out_ref[...] = jnp.zeros_like(out_ref)

    @pl.loop(2 * side // GROUP, tiles // GROUP)
    def _(step):
        here = pl.ds(pl.multiple_of(step * GROUP, GROUP), GROUP)
        messages = gather_group(src_ref[here, :], weight_ref[here, :], table_ref[...])
        out_ref[...] += scatter_group(dst_ref[here, :], messages, rows)


def local_sums(source, src_rows, weights, dst_rows, side, rows):
    return pl.pallas_call(
        functools.partial(local_kernel, side),
        out_shape=jax.ShapeDtypeStruct((rows, source.shape[1]), jnp.float32),
        in_specs=[VM] * 4,
        out_specs=VM,
        compiler_params=params(),
        cost_estimate=pl.CostEstimate(
            flops=8 * source.shape[0] * rows * 512, bytes_accessed=8 * 1024 * 1024, transcendentals=0
        ),
        name="local_sums",
    )(src_rows, weights, dst_rows, source)


def arrive_kernel(side, dst_ref, left_ref, right_ref, sums_ref, base_ref, out_ref):
    arrived = jnp.concatenate([left_ref[...], right_ref[...]], axis=0)
    total = scatter_group(dst_ref[: 2 * side], arrived, out_ref.shape[0])
    out_ref[...] = (base_ref[...].astype(jnp.float32) + (sums_ref[...] + total)).astype(out_ref.dtype)


def arrive_live_kernel(side, count_ref, dst_ref, left_ref, right_ref, sums_ref, base_ref, out_ref):
    arrived = jnp.concatenate([left_ref[...], right_ref[...]], axis=0)
    total = scatter_group(dst_ref[: 2 * side], arrived, out_ref.shape[0])
    total = base_ref[...].astype(jnp.float32) + (sums_ref[...] + total)
    live = lax.broadcasted_iota(jnp.int32, total.shape, 0) < count_ref[0]
    out_ref[...] = jnp.where(live, total, 0.0).astype(out_ref.dtype)


def arrivals(dst_rows, left, right, sums, base, side, count=None):
    kernel = arrive_kernel if count is None else arrive_live_kernel
    first = () if count is None else (count,)
    return pl.pallas_call(
        functools.partial(kernel, side),
        out_shape=jax.ShapeDtypeStruct(base.shape, base.dtype),
        in_specs=[pl.BlockSpec(memory_space=pltpu.SMEM)] * len(first) + [VM] * 5,
        out_specs=VM,
        compiler_params=params(),
        name="arrivals",
    )(*first, dst_rows, left, right, sums, base)


def both_ways(head, tail):
    count = lax.axis_size("seq")
    ends = count - 1
    left = lax.ppermute(tail, "seq", [(i, i + 1) for i in range(ends)])
    right = lax.ppermute(head, "seq", [(i + 1, i) for i in range(ends)])
    return left, right


def edges(source, src_rows, weights, dst_rows, base, side, count=None):
    sent = side_messages(source, src_rows, weights, side)
    width = side * TILE
    left, right = both_ways(sent[:width], sent[width:])
    sums = local_sums(source, src_rows, weights, dst_rows, side, base.shape[0])
    return arrivals(dst_rows, left, right, sums, base, side, count)


def qkv_kernel(x_ref, gain_ref, w_ref, normed_ref, q_ref, kv_ref):
    values = x_ref[...].astype(jnp.float32)
    centered = values - jnp.mean(values, axis=-1, keepdims=True)
    row_var = jnp.mean(centered * centered, axis=-1, keepdims=True)
    normed = (centered * lax.rsqrt(row_var + 1e-05) * gain_ref[...]).astype(jnp.bfloat16)
    normed_ref[...] = normed
    qkv = jnp.dot(normed, w_ref[...], preferred_element_type=jnp.float32).astype(jnp.bfloat16)
    blank = jnp.zeros((qkv.shape[0], HD), jnp.bfloat16)
    for head in range(qkv.shape[1] // (3 * HD)):
        at = head * 3 * HD
        query = qkv[:, at : at + HD] * HD ** (-0.5)
        q_ref[:, head * 2 * HD : (head + 1) * 2 * HD] = jnp.concatenate([query, blank], axis=1)
        kv_ref[:, head * 2 * HD : (head + 1) * 2 * HD] = qkv[:, at + HD : at + 3 * HD]


def qkv_rows(full_rows, norm_gain, w_qkv, block):
    rows, width = full_rows.shape
    wide = w_qkv.shape[1] // (3 * HD) * 2 * HD
    by_rows = lambda columns: pl.BlockSpec((block, columns), lambda i: (i, 0))
    whole = lambda array: pl.BlockSpec(array.shape, lambda i: (0, 0))
    return pl.pallas_call(
        qkv_kernel,
        grid=(rows // block,),
        out_shape=(
            jax.ShapeDtypeStruct((rows, width), jnp.bfloat16),
            jax.ShapeDtypeStruct((rows, wide), jnp.bfloat16),
            jax.ShapeDtypeStruct((rows, wide), jnp.bfloat16),
        ),
        in_specs=[by_rows(width), whole(norm_gain), whole(w_qkv)],
        out_specs=(by_rows(width), by_rows(wide), by_rows(wide)),
        compiler_params=params(),
        name="norm_qkv",
    )(full_rows, norm_gain, w_qkv)


def ffw_kernel(x_ref, up_ref, up_exp_ref, down_ref, down_exp_ref, out_ref):
    up = jnp.dot(x_ref[...], up_ref[...], preferred_element_type=jnp.float32)
    up = up * jnp.exp2(up_exp_ref[...].astype(jnp.float32))
    active = (0.5 * up * (1.0 + lax.erf(up * 0.5**0.5))).astype(jnp.bfloat16)
    down = jnp.dot(active, down_ref[...], preferred_element_type=jnp.float32)
    out_ref[...] = down * jnp.exp2(down_exp_ref[...].astype(jnp.float32))


def ffw_rows(normed, w_up, up_exp, w_down, down_exp, block):
    rows, width = normed.shape
    whole = lambda array: pl.BlockSpec(array.shape, lambda i: (0, 0))
    return pl.pallas_call(
        ffw_kernel,
        grid=(rows // block,),
        out_shape=jax.ShapeDtypeStruct((rows, w_down.shape[1]), jnp.float32),
        in_specs=[
            pl.BlockSpec((block, width), lambda i: (i, 0)),
            whole(w_up), whole(up_exp), whole(w_down), whole(down_exp),
        ],
        out_specs=pl.BlockSpec((block, w_down.shape[1]), lambda i: (i, 0)),
        compiler_params=params(),
        cost_estimate=pl.CostEstimate(
            flops=16 * rows * width * w_up.shape[1], bytes_accessed=16 * 1024 * 1024, transcendentals=0
        ),
        name="ffw",
    )(normed, w_up, up_exp, w_down, down_exp)


def attention_kernel(block, q_ref, left_ref, kv_ref, right_ref, w_ref, mlp_ref, out_ref):
    step = pl.program_id(0)
    rows = kv_ref.shape[0]
    me = lax.axis_index("seq")
    total_rows = rows * lax.axis_size("seq")
    heads = q_ref.shape[1] // (2 * HD)
    start = step * block
    pieces = (block + 2 * WIN) // block
    row = lax.broadcasted_iota(jnp.int32, (block, block), 0)
    lane = lax.broadcasted_iota(jnp.int32, (block, block), 1)
    front = lax.broadcasted_iota(jnp.int32, (block, 2 * HD), 1) < HD
    outs = []
    for head in range(heads):
        columns = slice(head * 2 * HD, (head + 1) * 2 * HD)
        query = q_ref[pl.ds(start, block), columns]
        parts, windows = [], []
        for piece in range(pieces):
            at = start + (piece * block - WIN)
            inside = pl.ds(pl.multiple_of(jnp.clip(at, 0, rows - block), block), block)
            before = pl.ds(pl.multiple_of(jnp.clip(at + WIN, 0, WIN - block), block), block)
            after = pl.ds(pl.multiple_of(jnp.clip(at - rows, 0, WIN - block), block), block)
            window = kv_ref[inside, columns]
            if piece * block < WIN:
                window = jnp.where(at < 0, left_ref[before, columns], window)
            if piece * block > WIN:
                window = jnp.where(at >= rows, right_ref[after, columns], window)
            windows.append(jnp.where(front, jnp.bfloat16(1), window))
            part = lax.dot_general(
                query, window, (((1,), (1,)), ((), ())), preferred_element_type=jnp.float32
            )
            if piece * block != WIN:
                here = me * rows + at
                part = part + jnp.where((here >= 0) & (here < total_rows), 0.0, -1e30)
            if piece == 0:
                part = jnp.where(lane >= row, part, -1e30)
            if piece == pieces - 1:
                part = jnp.where(lane <= row, part, -1e30)
            parts.append(part)
        scores = jnp.concatenate(parts, axis=1)
        peak = jnp.max(scores, axis=-1, keepdims=True)
        probs = jnp.exp(scores - peak).astype(jnp.bfloat16)
        mixed = jnp.dot(probs, jnp.concatenate(windows, axis=0), preferred_element_type=jnp.float32)
        rolled = pltpu.roll(mixed, HD, 1)
        outs.append(rolled / mixed if head % 2 == 0 else mixed / rolled)
    pairs = [jnp.where(front, outs[i], outs[i + 1]) for i in range(0, heads, 2)]
    attended = jnp.concatenate(pairs, axis=1).astype(jnp.bfloat16)
    out = jnp.dot(attended, w_ref[...], preferred_element_type=jnp.float32) + mlp_ref[...]
    out_ref[...] = out.astype(jnp.bfloat16)


def attention(queries, left, kv, right, w_out, mlp_part, block):
    rows = kv.shape[0]
    whole = lambda array: pl.BlockSpec(array.shape, lambda i: (0, 0))
    wide = w_out.shape[1]
    return pl.pallas_call(
        functools.partial(attention_kernel, block),
        grid=(rows // block,),
        out_shape=jax.ShapeDtypeStruct((rows, wide), jnp.bfloat16),
        in_specs=[whole(queries), whole(left), whole(kv), whole(right), whole(w_out),
                  pl.BlockSpec((block, wide), lambda i: (i, 0))],
        out_specs=pl.BlockSpec((block, wide), lambda i: (i, 0)),
        compiler_params=params(),
        name="attention",
    )(queries, left, kv, right, w_out, mlp_part)


def shards(
    grid_latent, grid_count, hidden_embed, enc_src_rows, enc_dst_rows, enc_weight,
    dec_src_rows, dec_dst_rows, dec_weight, norm_gain, w_qkv, w_out, w_up, up_exp, w_down, down_exp,
):
    block = 256
    latent = edges(
        grid_latent, enc_src_rows[0], enc_weight[0], enc_dst_rows[0], hidden_embed, ESIDE
    )
    full_rows = lax.all_gather(latent, ("mp", "sub"), axis=1, tiled=True)
    normed, queries, kv = qkv_rows(full_rows, norm_gain[None, :], w_qkv, block)
    left, right = both_ways(kv[:WIN], kv[kv.shape[0] - WIN :])
    mlp_part = ffw_rows(normed, w_up, up_exp[None, :], w_down, down_exp[None, :], block)
    partial = attention(queries, left, kv, right, w_out, mlp_part, block)
    summed = lax.psum_scatter(
        partial, ("mp", "sub"), scatter_dimension=1, tiled=True
    ).astype(jnp.float32)
    hidden_out = (latent.astype(jnp.float32) + summed).astype(jnp.bfloat16)
    grid_out = edges(
        hidden_out, dec_src_rows[0], dec_weight[0], dec_dst_rows[0], grid_latent, DSIDE, grid_count
    )
    return (hidden_out, grid_out)


def solution(mesh):
    rows = P(("ens", "seq"), ("mp", "sub"))
    tiles = P(("ens", "seq"), None, None)
    across, down = P(None, ("mp", "sub")), P(("mp", "sub"), None)
    placed = (
        rows, P(("ens", "seq")), rows, tiles, tiles, tiles, tiles, tiles, tiles,
        P(), across, down, across, P(("mp", "sub")), down, P(),
    )
    return jax.shard_map(shards, mesh=mesh, in_specs=placed, out_specs=(rows, rows), check_vma=False)
```

```python
import functools

import jax
import jax.numpy as jnp
from jax import lax
from jax.experimental import pallas as pl
from jax.experimental.pallas import tpu as pltpu
from jax.sharding import PartitionSpec as P

HD = 64
WIN = 512
TILE = 128
ESIDE = 4
DSIDE = 4
GROUP = 8
BLOCK = 256
LIMIT = 60 * 1024 * 1024
VM = pl.BlockSpec(memory_space=pltpu.VMEM)
DMA = pltpu.SemaphoreType.DMA
MESH = pl.DeviceIdType.MESH


def turned(row):
    return jnp.broadcast_to(row, (TILE, TILE)).T


def gather_group(src, weight, table):
    rows, columns = table.shape
    lane = lax.broadcasted_iota(jnp.int32, (TILE, rows), 1).astype(jnp.int16)
    picks, scales = [], []
    for tile in range(src.shape[0]):
        col = turned(src[tile : tile + 1]).astype(jnp.int16)
        col = jnp.concatenate([col] * (rows // TILE), axis=1)
        picks.append(jnp.where(lane == col, jnp.bfloat16(1), jnp.bfloat16(0)))
        scale = turned(weight[tile : tile + 1])
        scales.append(jnp.concatenate([scale] * (columns // TILE), axis=1))
    picked = jnp.dot(jnp.concatenate(picks, axis=0), table, preferred_element_type=jnp.float32)
    return (picked * jnp.concatenate(scales, axis=0)).astype(jnp.bfloat16)


def scatter_group(dst, messages, rows, first=0):
    line = lax.broadcasted_iota(jnp.int32, (rows, TILE), 0).astype(jnp.int16)
    spots = []
    for tile in range(dst.shape[0]):
        row = jnp.broadcast_to(dst[tile : tile + 1] - first, (16, TILE)).astype(jnp.int16)
        row = jnp.concatenate([row] * (rows // 16), axis=0)
        spots.append(jnp.where(line == row, jnp.bfloat16(1), jnp.bfloat16(0)))
    return jnp.dot(jnp.concatenate(spots, axis=1), messages, preferred_element_type=jnp.float32)


def remote(src, dst, send, recv, **where):
    return pltpu.make_async_remote_copy(
        src_ref=src, dst_ref=dst, send_sem=send, recv_sem=recv, device_id=where, device_id_type=MESH
    )


def greet(peers):
    me, ends = lax.axis_index("seq"), lax.axis_size("seq") - 1
    barrier = pltpu.get_barrier_semaphore()
    for peer in peers:
        pl.semaphore_signal(barrier, inc=1, device_id=peer, device_id_type=MESH)

    @pl.when(me > 0)
    def _():
        pl.semaphore_signal(barrier, inc=1, device_id={"seq": me - 1}, device_id_type=MESH)

    @pl.when(me < ends)
    def _():
        pl.semaphore_signal(barrier, inc=1, device_id={"seq": me + 1}, device_id_type=MESH)

    near = jnp.where(me > 0, 1, 0) + jnp.where(me < ends, 1, 0)
    pl.semaphore_wait(barrier, near + len(peers))


def edge_sums(side, src_ref, weight_ref, dst_ref, table_ref, sums, sent, arrived, send, recv):
    me, ends = lax.axis_index("seq"), lax.axis_size("seq") - 1
    width = side * TILE
    rows = sums.shape[0]
    head, tail = pl.ds(0, width), pl.ds(width, width)
    to_left = remote(sent.at[head], arrived.at[tail], send.at[0], recv.at[0], seq=me - 1)
    to_right = remote(sent.at[tail], arrived.at[head], send.at[1], recv.at[1], seq=me + 1)
    sent[...] = gather_group(src_ref[: 2 * side], weight_ref[: 2 * side], table_ref[...])

    @pl.when(me > 0)
    def _():
        to_left.start()

    @pl.when(me < ends)
    def _():
        to_right.start()

    sums[...] = jnp.zeros_like(sums)

    @pl.loop(2 * side // GROUP, src_ref.shape[0] // GROUP)
    def _(step):
        here = pl.ds(pl.multiple_of(step * GROUP, GROUP), GROUP)
        messages = gather_group(src_ref[here, :], weight_ref[here, :], table_ref[...])
        sums[...] += scatter_group(dst_ref[here, :], messages, rows)

    @pl.when(me > 0)
    def _():
        to_right.wait_recv()

    @pl.when(me == 0)
    def _():
        arrived[head] = jnp.zeros((width, arrived.shape[1]), arrived.dtype)

    @pl.when(me < ends)
    def _():
        to_left.wait_recv()

    @pl.when(me == ends)
    def _():
        arrived[tail] = jnp.zeros((width, arrived.shape[1]), arrived.dtype)

    def finish():
        @pl.when(me > 0)
        def _():
            to_left.wait_send()

        @pl.when(me < ends)
        def _():
            to_right.wait_send()

    return finish


def layer_kernel(
    src_ref, weight_ref, dst_ref, grid_ref, embed_ref, gain_ref, up_exp_ref, down_exp_ref,
    qkv_hbm, up_hbm, down_hbm, out_hbm, hidden_ref,
    sums, sent, arrived, full, normed, queries, kv, mlp, parts, in1, out2, in2,
    w_qkv, w_up, w_down, w_out,
    w_sem, z_send, z_recv, ax_send, ax_recv, as_send, as_recv, kv_send, kv_recv,
    r1_send, r1_recv, r2_send, r2_recv,
):
    me, ends = lax.axis_index("seq"), lax.axis_size("seq") - 1
    mp, n_mp = lax.axis_index("mp"), lax.axis_size("mp")
    sub, n_sub = lax.axis_index("sub"), lax.axis_size("sub")
    rows, columns = embed_ref.shape
    blocks = n_mp * n_sub
    chunks = rows // BLOCK
    heads = queries.shape[1] // (2 * HD)
    own = mp * n_sub + sub

    loads = [
        pltpu.make_async_copy(src, dst, w_sem.at[i])
        for i, (src, dst) in enumerate(
            ((qkv_hbm, w_qkv), (up_hbm, w_up), (down_hbm, w_down), (out_hbm, w_out))
        )
    ]
    for load in loads:
        load.start()

    mp_at = lambda j: lax.rem(mp + j, n_mp)
    sub_at = lambda k: lax.rem(sub + k, n_sub)
    greet([{"mp": mp_at(j)} for j in range(1, n_mp)] + [{"sub": sub_at(k)} for k in range(1, n_sub)])

    def at_rows(chunk):
        return pl.ds(pl.multiple_of(chunk * BLOCK, BLOCK), BLOCK)

    def gather_mp(chunk, j, owner):
        piece = full.at[owner, at_rows(chunk)]
        return remote(piece, piece, ax_send.at[j - 1, chunk], ax_recv.at[j - 1, chunk], mp=mp_at(j))

    def gather_sub(chunk, k, j, owner):
        piece = full.at[owner, at_rows(chunk)]
        return remote(
            piece, piece, as_send.at[k - 1, j, chunk], as_recv.at[k - 1, j, chunk], sub=sub_at(k)
        )

    from_mp = lambda j: lax.rem(mp + n_mp - j, n_mp)
    from_sub = lambda k: lax.rem(sub + n_sub - k, n_sub)

    finish_edges = edge_sums(
        ESIDE, src_ref, weight_ref, dst_ref, grid_ref, sums, sent, arrived, z_send, z_recv
    )

    @pl.loop(0, chunks)
    def _(chunk):
        here = at_rows(chunk)
        total = scatter_group(dst_ref[: 2 * ESIDE], arrived[...], BLOCK, chunk * BLOCK)
        latent = embed_ref[here, :].astype(jnp.float32) + (sums[here, :] + total)
        full[own, here] = latent.astype(jnp.bfloat16)
        for j in range(1, n_mp):
            gather_mp(chunk, j, own).start()
        for k in range(1, n_sub):
            gather_sub(chunk, k, 0, own).start()

    def forward(chunk):
        for j in range(1, n_mp):
            owner = from_mp(j) * n_sub + sub
            gather_mp(chunk, j, owner).wait_recv()
            for k in range(1, n_sub):
                gather_sub(chunk, k, j, owner).start()

    def kv_copy(chunk, way):
        src = kv.at[pl.ds(pl.multiple_of(WIN + chunk * BLOCK, BLOCK), BLOCK)]
        shift = WIN + rows if way == 0 else WIN - rows
        dst = kv.at[pl.ds(pl.multiple_of(shift + chunk * BLOCK, BLOCK), BLOCK)]
        to = me - 1 if way == 0 else me + 1
        return remote(src, dst, kv_send.at[way, chunk], kv_recv.at[way, chunk], seq=to)

    to_left = range(WIN // BLOCK)
    to_right = range((rows - WIN) // BLOCK, chunks)

    def project(chunk):
        here = at_rows(chunk)
        for k in range(1, n_sub):
            for j in range(n_mp):
                owner = (from_mp(j) if j else mp) * n_sub + from_sub(k)
                gather_sub(chunk, k, j, owner).wait_recv()
        values = jnp.concatenate([full[t, here] for t in range(blocks)], axis=1).astype(jnp.float32)
        centered = values - jnp.mean(values, axis=-1, keepdims=True)
        row_var = jnp.mean(centered * centered, axis=-1, keepdims=True)
        rows_normed = (centered * lax.rsqrt(row_var + 1e-05) * gain_ref[...]).astype(jnp.bfloat16)
        normed[here, :] = rows_normed
        qkv = jnp.dot(rows_normed, w_qkv[...], preferred_element_type=jnp.float32)
        qkv = qkv.astype(jnp.bfloat16)
        blank = jnp.zeros((BLOCK, HD), jnp.bfloat16)
        inner = pl.ds(pl.multiple_of(WIN + chunk * BLOCK, BLOCK), BLOCK)
        for head in range(heads):
            at = head * 3 * HD
            wide = slice(head * 2 * HD, (head + 1) * 2 * HD)
            query = qkv[:, at : at + HD] * HD ** (-0.5)
            queries[here, wide] = jnp.concatenate([query, blank], axis=1)
            kv[inner, wide] = qkv[:, at + HD : at + 3 * HD]

        @pl.when((me > 0) & (chunk < to_left.stop))
        def _():
            kv_copy(chunk, 0).start()

        @pl.when((me < ends) & (chunk >= to_right.start))
        def _():
            kv_copy(chunk, 1).start()

    def feed_forward(chunk):
        here = at_rows(chunk)
        up = jnp.dot(normed[here, :], w_up[...], preferred_element_type=jnp.float32)
        up = up * jnp.exp2(up_exp_ref[...].astype(jnp.float32))
        active = (0.5 * up * (1.0 + lax.erf(up * 0.5**0.5))).astype(jnp.bfloat16)
        down = jnp.dot(active, w_down[...], preferred_element_type=jnp.float32)
        mlp[here, :] = down * jnp.exp2(down_exp_ref[...].astype(jnp.float32))

    edge_rows = jnp.zeros((WIN, kv.shape[1]), kv.dtype)

    @pl.when(me == 0)
    def _():
        kv[pl.ds(0, WIN)] = edge_rows

    @pl.when(me == ends)
    def _():
        kv[pl.ds(WIN + rows, WIN)] = edge_rows

    for load in loads:
        load.wait()
    forward(0)

    @pl.loop(0, chunks)
    def _(chunk):
        project(chunk)

        @pl.when(chunk + 1 < chunks)
        def _():
            forward(chunk + 1)

    @pl.loop(0, chunks)
    def _(chunk):
        feed_forward(chunk)

    @pl.when(me > 0)
    def _():
        for chunk in to_right:
            kv_copy(chunk, 1).wait_recv()

    @pl.when(me < ends)
    def _():
        for chunk in to_left:
            kv_copy(chunk, 0).wait_recv()

    def scatter_sub(chunk, k, m):
        return remote(
            parts.at[chunk, m * n_sub + sub_at(k)], in1.at[chunk, k - 1, m],
            r1_send.at[chunk, k - 1, m], r1_recv.at[chunk, k - 1, m], sub=sub_at(k),
        )

    def scatter_mp(chunk, j):
        return remote(
            out2.at[chunk, j - 1], in2.at[chunk, j - 1],
            r2_send.at[chunk, j - 1], r2_recv.at[chunk, j - 1], mp=mp_at(j),
        )

    pieces = (BLOCK + 2 * WIN) // BLOCK
    row = lax.broadcasted_iota(jnp.int32, (BLOCK, BLOCK), 0)
    lane = lax.broadcasted_iota(jnp.int32, (BLOCK, BLOCK), 1)
    front = lax.broadcasted_iota(jnp.int32, (BLOCK, 2 * HD), 1) < HD

    def attend(chunk):
        here = at_rows(chunk)
        outs = []
        for head in range(heads):
            wide = slice(head * 2 * HD, (head + 1) * 2 * HD)
            query = queries[here, wide]
            scored, windows = [], []
            for piece in range(pieces):
                at = pl.multiple_of(chunk * BLOCK + piece * BLOCK, BLOCK)
                window = kv[pl.ds(at, BLOCK), wide]
                windows.append(jnp.where(front, jnp.bfloat16(1), window))
                part = lax.dot_general(
                    query, window, (((1,), (1,)), ((), ())), preferred_element_type=jnp.float32
                )
                if piece * BLOCK != WIN:
                    spot = me * rows + at - WIN
                    inside = (spot >= 0) & (spot < (ends + 1) * rows)
                    part = part + jnp.where(inside, 0.0, -1e30)
                if piece == 0:
                    part = jnp.where(lane >= row, part, -1e30)
                if piece == pieces - 1:
                    part = jnp.where(lane <= row, part, -1e30)
                scored.append(part)
            scores = jnp.concatenate(scored, axis=1)
            peak = jnp.max(scores, axis=-1, keepdims=True)
            probs = jnp.exp(scores - peak).astype(jnp.bfloat16)
            mixed = jnp.dot(
                probs, jnp.concatenate(windows, axis=0), preferred_element_type=jnp.float32
            )
            rolled = pltpu.roll(mixed, HD, 1)
            outs.append(rolled / mixed if head % 2 == 0 else mixed / rolled)
        pairs = [jnp.where(front, outs[i], outs[i + 1]) for i in range(0, heads, 2)]
        attended = jnp.concatenate(pairs, axis=1).astype(jnp.bfloat16)
        out = jnp.dot(attended, w_out[...], preferred_element_type=jnp.float32) + mlp[here, :]
        out = out.astype(jnp.bfloat16)
        for t in range(blocks):
            parts[chunk, t] = out[:, t * columns : (t + 1) * columns]
        for k in range(1, n_sub):
            for m in range(n_mp):
                scatter_sub(chunk, k, m).start()

    def chip_sum(chunk, m):
        total = parts[chunk, m * n_sub + sub].astype(jnp.float32)
        for k in range(1, n_sub):
            total += in1[chunk, k - 1, m].astype(jnp.float32)
        return total

    def pass_on(chunk):
        for k in range(1, n_sub):
            for m in range(n_mp):
                scatter_sub(chunk, k, m).wait_recv()
        for j in range(1, n_mp):
            out2[chunk, j - 1] = chip_sum(chunk, mp_at(j)).astype(jnp.bfloat16)
            scatter_mp(chunk, j).start()

    @pl.loop(0, chunks)
    def _(chunk):
        attend(chunk)

        @pl.when(chunk > 0)
        def _():
            pass_on(chunk - 1)

    pass_on(chunks - 1)

    @pl.loop(0, chunks)
    def _(chunk):
        here = at_rows(chunk)
        total = chip_sum(chunk, mp)
        for j in range(1, n_mp):
            scatter_mp(chunk, j).wait_recv()
            total += in2[chunk, j - 1].astype(jnp.float32)
        hidden_ref[here, :] = (full[own, here].astype(jnp.float32) + total).astype(jnp.bfloat16)

    finish_edges()

    @pl.loop(0, chunks)
    def _(chunk):
        for j in range(1, n_mp):
            gather_mp(chunk, j, own).wait_send()
            scatter_mp(chunk, j).wait_send()
        for k in range(1, n_sub):
            for j in range(n_mp):
                gather_sub(chunk, k, j, own).wait_send()
                scatter_sub(chunk, k, j).wait_send()

    @pl.when(me > 0)
    def _():
        for chunk in to_left:
            kv_copy(chunk, 0).wait_send()

    @pl.when(me < ends)
    def _():
        for chunk in to_right:
            kv_copy(chunk, 1).wait_send()


def layer(src, weight, dst, grid, embed, gain, up_exp, down_exp, w_qkv, w_up, w_down, w_out):
    rows, columns = embed.shape
    n_mp, n_sub = lax.axis_size("mp"), lax.axis_size("sub")
    blocks, chunks = n_mp * n_sub, rows // BLOCK
    wide = w_qkv.shape[1] // (3 * HD) * 2 * HD
    half = lambda *shape: pltpu.VMEM(shape, jnp.bfloat16)
    full = lambda *shape: pltpu.VMEM(shape, jnp.float32)
    side = 2 * ESIDE * TILE
    return pl.pallas_call(
        layer_kernel,
        out_shape=jax.ShapeDtypeStruct((rows, columns), jnp.bfloat16),
        in_specs=[VM] * 8 + [pl.BlockSpec(memory_space=pl.ANY)] * 4,
        out_specs=VM,
        scratch_shapes=[
            full(rows, columns), half(side, columns), half(side, columns),
            half(blocks, rows, columns), half(rows, w_qkv.shape[0]),
            half(rows, wide), half(rows + 2 * WIN, wide), full(rows, w_down.shape[1]),
            half(chunks, blocks, BLOCK, columns), half(chunks, n_sub - 1, n_mp, BLOCK, columns),
            half(chunks, n_mp - 1, BLOCK, columns), half(chunks, n_mp - 1, BLOCK, columns),
            half(*w_qkv.shape), half(*w_up.shape), half(*w_down.shape), half(*w_out.shape),
            DMA((4,)), DMA((2,)), DMA((2,)),
            DMA((n_mp - 1, chunks)), DMA((n_mp - 1, chunks)),
            DMA((n_sub - 1, n_mp, chunks)), DMA((n_sub - 1, n_mp, chunks)),
            DMA((2, chunks)), DMA((2, chunks)),
            DMA((chunks, n_sub - 1, n_mp)), DMA((chunks, n_sub - 1, n_mp)),
            DMA((chunks, n_mp - 1)), DMA((chunks, n_mp - 1)),
        ],
        compiler_params=pltpu.CompilerParams(
            vmem_limit_bytes=LIMIT, collective_id=0, has_side_effects=True
        ),
        name="encode_layer",
    )(src, weight, dst, grid, embed, gain, up_exp, down_exp, w_qkv, w_up, w_down, w_out)


def decode_kernel(
    count_ref, src_ref, weight_ref, dst_ref, table_ref, base_ref, out_ref,
    sums, sent, arrived, z_send, z_recv,
):
    greet([])
    finish = edge_sums(
        DSIDE, src_ref, weight_ref, dst_ref, table_ref, sums, sent, arrived, z_send, z_recv
    )
    total = scatter_group(dst_ref[: 2 * DSIDE], arrived[...], out_ref.shape[0])
    total = base_ref[...].astype(jnp.float32) + (sums[...] + total)
    live = lax.broadcasted_iota(jnp.int32, total.shape, 0) < count_ref[0]
    out_ref[...] = jnp.where(live, total, 0.0).astype(out_ref.dtype)
    finish()


def decode(count, src, weight, dst, table, base):
    side = 2 * DSIDE * TILE
    columns = base.shape[1]
    return pl.pallas_call(
        decode_kernel,
        out_shape=jax.ShapeDtypeStruct(base.shape, base.dtype),
        in_specs=[pl.BlockSpec(memory_space=pltpu.SMEM)] + [VM] * 5,
        out_specs=VM,
        scratch_shapes=[
            pltpu.VMEM(base.shape, jnp.float32),
            pltpu.VMEM((side, columns), jnp.bfloat16),
            pltpu.VMEM((side, columns), jnp.bfloat16),
            DMA((2,)), DMA((2,)),
        ],
        compiler_params=pltpu.CompilerParams(
            vmem_limit_bytes=LIMIT, collective_id=1, has_side_effects=True
        ),
        name="decode",
    )(count, src, weight, dst, table, base)


def shards(
    grid_latent, grid_count, hidden_embed, enc_src_rows, enc_dst_rows, enc_weight,
    dec_src_rows, dec_dst_rows, dec_weight, norm_gain, w_qkv, w_out, w_up, up_exp, w_down, down_exp,
):
    hidden_out = layer(
        enc_src_rows[0], enc_weight[0], enc_dst_rows[0], grid_latent, hidden_embed,
        norm_gain[None, :], up_exp[None, :], down_exp[None, :], w_qkv, w_up, w_down, w_out,
    )
    grid_out = decode(
        grid_count, dec_src_rows[0], dec_weight[0], dec_dst_rows[0], hidden_out, grid_latent
    )
    return (hidden_out, grid_out)


def solution(mesh):
    rows = P(("ens", "seq"), ("mp", "sub"))
    tiles = P(("ens", "seq"), None, None)
    across, down = P(None, ("mp", "sub")), P(("mp", "sub"), None)
    placed = (
        rows, P(("ens", "seq")), rows, tiles, tiles, tiles, tiles, tiles, tiles,
        P(), across, down, across, P(("mp", "sub")), down, P(),
    )
    return jax.shard_map(shards, mesh=mesh, in_specs=placed, out_specs=(rows, rows), check_vma=False)
```

```python
import functools

import jax
import jax.numpy as jnp
from jax import lax
from jax.experimental import pallas as pl
from jax.experimental.pallas import tpu as pltpu
from jax.sharding import PartitionSpec as P

HD = 64
WIN = 512
TILE = 128
ESIDE = 4
DSIDE = 4
GROUP = 8
BLOCK = 256
LIMIT = 60 * 1024 * 1024
VM = pl.BlockSpec(memory_space=pltpu.VMEM)
DMA = pltpu.SemaphoreType.DMA
MESH = pl.DeviceIdType.MESH


def turned(row):
    return jnp.broadcast_to(row, (TILE, TILE)).T


def gather_group(src, weight, table):
    rows, columns = table.shape
    lane = lax.broadcasted_iota(jnp.int32, (TILE, rows), 1).astype(jnp.int16)
    picks, scales = [], []
    for tile in range(src.shape[0]):
        col = turned(src[tile : tile + 1]).astype(jnp.int16)
        col = jnp.concatenate([col] * (rows // TILE), axis=1)
        picks.append(jnp.where(lane == col, jnp.bfloat16(1), jnp.bfloat16(0)))
        scale = turned(weight[tile : tile + 1])
        scales.append(jnp.concatenate([scale] * (columns // TILE), axis=1))
    picked = jnp.dot(jnp.concatenate(picks, axis=0), table, preferred_element_type=jnp.float32)
    return (picked * jnp.concatenate(scales, axis=0)).astype(jnp.bfloat16)


def scatter_group(dst, messages, rows, first=0):
    line = lax.broadcasted_iota(jnp.int32, (rows, TILE), 0).astype(jnp.int16)
    spots = []
    for tile in range(dst.shape[0]):
        row = jnp.broadcast_to(dst[tile : tile + 1] - first, (16, TILE)).astype(jnp.int16)
        row = jnp.concatenate([row] * (rows // 16), axis=0)
        spots.append(jnp.where(line == row, jnp.bfloat16(1), jnp.bfloat16(0)))
    return jnp.dot(jnp.concatenate(spots, axis=1), messages, preferred_element_type=jnp.float32)


def remote(src, dst, send, recv, **where):
    return pltpu.make_async_remote_copy(
        src_ref=src, dst_ref=dst, send_sem=send, recv_sem=recv, device_id=where, device_id_type=MESH
    )


def greet(peers):
    me, ends = lax.axis_index("seq"), lax.axis_size("seq") - 1
    barrier = pltpu.get_barrier_semaphore()
    for peer in peers:
        pl.semaphore_signal(barrier, inc=1, device_id=peer, device_id_type=MESH)

    @pl.when(me > 0)
    def _():
        pl.semaphore_signal(barrier, inc=1, device_id={"seq": me - 1}, device_id_type=MESH)

    @pl.when(me < ends)
    def _():
        pl.semaphore_signal(barrier, inc=1, device_id={"seq": me + 1}, device_id_type=MESH)

    near = jnp.where(me > 0, 1, 0) + jnp.where(me < ends, 1, 0)
    pl.semaphore_wait(barrier, near + len(peers))


def edge_messages(side, src_ref, weight_ref, table_ref, sent, messages, send, recv, greeting=None):
    me, ends = lax.axis_index("seq"), lax.axis_size("seq") - 1
    width = side * TILE
    head, tail = pl.ds(0, width), pl.ds(width, width)
    to_left = remote(sent.at[head], messages.at[tail], send.at[0], recv.at[0], seq=me - 1)
    to_right = remote(sent.at[tail], messages.at[head], send.at[1], recv.at[1], seq=me + 1)
    sent[...] = gather_group(src_ref[: 2 * side], weight_ref[: 2 * side], table_ref[...])
    if greeting is not None:
        greet(greeting)

    @pl.when(me > 0)
    def _():
        to_left.start()

    @pl.when(me < ends)
    def _():
        to_right.start()

    @pl.loop(2 * side // GROUP, src_ref.shape[0] // GROUP)
    def _(step):
        here = pl.ds(pl.multiple_of(step * GROUP, GROUP), GROUP)
        spots = pl.ds(pl.multiple_of(step * GROUP * TILE, GROUP * TILE), GROUP * TILE)
        messages[spots, :] = gather_group(src_ref[here, :], weight_ref[here, :], table_ref[...])

    @pl.when(me > 0)
    def _():
        to_right.wait_recv()

    @pl.when(me == 0)
    def _():
        messages[head] = jnp.zeros((width, messages.shape[1]), messages.dtype)

    @pl.when(me < ends)
    def _():
        to_left.wait_recv()

    @pl.when(me == ends)
    def _():
        messages[tail] = jnp.zeros((width, messages.shape[1]), messages.dtype)

    def finish():
        @pl.when(me > 0)
        def _():
            to_left.wait_send()

        @pl.when(me < ends)
        def _():
            to_right.wait_send()

    return finish


def layer_kernel(
    count_ref, src_ref, weight_ref, dst_ref, dec_src_ref, dec_weight_ref, dec_dst_ref,
    grid_ref, embed_ref, gain_ref, up_exp_ref, down_exp_ref,
    qkv_hbm, up_hbm, down_hbm, out_hbm, hidden_ref, result_ref,
    sent, messages, dec_sent, dec_messages, full, normed, queries, kv, mlp, parts, in1, out2, in2,
    w_qkv, w_up, w_down, w_out,
    w_sem, z_send, z_recv, d_send, d_recv, ax_send, ax_recv, as_send, as_recv, kv_send, kv_recv,
    r1_send, r1_recv, r2_send, r2_recv,
):
    me, ends = lax.axis_index("seq"), lax.axis_size("seq") - 1
    mp, n_mp = lax.axis_index("mp"), lax.axis_size("mp")
    sub, n_sub = lax.axis_index("sub"), lax.axis_size("sub")
    rows, columns = embed_ref.shape
    blocks = n_mp * n_sub
    chunks = rows // BLOCK
    heads = queries.shape[1] // (2 * HD)
    own = mp * n_sub + sub

    loads = [
        pltpu.make_async_copy(src, dst, w_sem.at[i])
        for i, (src, dst) in enumerate(
            ((qkv_hbm, w_qkv), (up_hbm, w_up), (down_hbm, w_down), (out_hbm, w_out))
        )
    ]
    for load in loads:
        load.start()

    mp_at = lambda j: lax.rem(mp + j, n_mp)
    sub_at = lambda k: lax.rem(sub + k, n_sub)
    peers = [{"mp": mp_at(j)} for j in range(1, n_mp)] + [{"sub": sub_at(k)} for k in range(1, n_sub)]

    def at_rows(chunk):
        return pl.ds(pl.multiple_of(chunk * BLOCK, BLOCK), BLOCK)

    def gather_mp(chunk, j, owner):
        piece = full.at[owner, at_rows(chunk)]
        return remote(piece, piece, ax_send.at[j - 1, chunk], ax_recv.at[j - 1, chunk], mp=mp_at(j))

    def gather_sub(chunk, k, j, owner):
        piece = full.at[owner, at_rows(chunk)]
        return remote(
            piece, piece, as_send.at[k - 1, j, chunk], as_recv.at[k - 1, j, chunk], sub=sub_at(k)
        )

    from_mp = lambda j: lax.rem(mp + n_mp - j, n_mp)
    from_sub = lambda k: lax.rem(sub + n_sub - k, n_sub)

    finish_edges = edge_messages(
        ESIDE, src_ref, weight_ref, grid_ref, sent, messages, z_send, z_recv, peers
    )

    def turn(step):
        return step % 2 * (chunks // 2) + step // 2 if chunks % 2 == 0 else step

    @pl.loop(0, chunks)
    def _(step):
        chunk = turn(step)
        here = at_rows(chunk)
        total = scatter_group(dst_ref[...], messages[...], BLOCK, chunk * BLOCK)
        latent = embed_ref[here, :].astype(jnp.float32) + total
        full[own, here] = latent.astype(jnp.bfloat16)
        for j in range(1, n_mp):
            gather_mp(chunk, j, own).start()
        for k in range(1, n_sub):
            gather_sub(chunk, k, 0, own).start()

    def forward(chunk):
        for j in range(1, n_mp):
            owner = from_mp(j) * n_sub + sub
            gather_mp(chunk, j, owner).wait_recv()
            for k in range(1, n_sub):
                gather_sub(chunk, k, j, owner).start()

    def kv_copy(chunk, way):
        src = kv.at[pl.ds(pl.multiple_of(WIN + chunk * BLOCK, BLOCK), BLOCK)]
        shift = WIN + rows if way == 0 else WIN - rows
        dst = kv.at[pl.ds(pl.multiple_of(shift + chunk * BLOCK, BLOCK), BLOCK)]
        to = me - 1 if way == 0 else me + 1
        return remote(src, dst, kv_send.at[way, chunk], kv_recv.at[way, chunk], seq=to)

    to_left = range(WIN // BLOCK)
    to_right = range((rows - WIN) // BLOCK, chunks)

    def project(chunk):
        here = at_rows(chunk)
        for k in range(1, n_sub):
            for j in range(n_mp):
                owner = (from_mp(j) if j else mp) * n_sub + from_sub(k)
                gather_sub(chunk, k, j, owner).wait_recv()
        values = jnp.concatenate([full[t, here] for t in range(blocks)], axis=1).astype(jnp.float32)
        centered = values - jnp.mean(values, axis=-1, keepdims=True)
        row_var = jnp.mean(centered * centered, axis=-1, keepdims=True)
        rows_normed = (centered * lax.rsqrt(row_var + 1e-05) * gain_ref[...]).astype(jnp.bfloat16)
        normed[here, :] = rows_normed
        qkv = jnp.dot(rows_normed, w_qkv[...], preferred_element_type=jnp.float32)
        qkv = qkv.astype(jnp.bfloat16)
        blank = jnp.zeros((BLOCK, HD), jnp.bfloat16)
        inner = pl.ds(pl.multiple_of(WIN + chunk * BLOCK, BLOCK), BLOCK)
        for head in range(heads):
            at = head * 3 * HD
            wide = slice(head * 2 * HD, (head + 1) * 2 * HD)
            query = qkv[:, at : at + HD] * HD ** (-0.5)
            queries[here, wide] = jnp.concatenate([query, blank], axis=1)
            kv[inner, wide] = qkv[:, at + HD : at + 3 * HD]

        @pl.when((me > 0) & (chunk < to_left.stop))
        def _():
            kv_copy(chunk, 0).start()

        @pl.when((me < ends) & (chunk >= to_right.start))
        def _():
            kv_copy(chunk, 1).start()

    def feed_forward(chunk):
        here = at_rows(chunk)
        rows_normed = normed[here, :]
        units = w_up.shape[1]
        width = min(256, units)

        def rise(at):
            return jnp.dot(
                rows_normed, w_up[:, at : at + width], preferred_element_type=jnp.float32
            )

        later, pieces = rise(0), []
        for at in range(0, units, width):
            up, later = later, rise(at + width) if at + width < units else None
            up = up * jnp.exp2(up_exp_ref[:, at : at + width].astype(jnp.float32))
            pieces.append((0.5 * up * (1.0 + lax.erf(up * 0.5**0.5))).astype(jnp.bfloat16))
        active = jnp.concatenate(pieces, axis=1)
        down = jnp.dot(active, w_down[...], preferred_element_type=jnp.float32)
        mlp[here, :] = down * jnp.exp2(down_exp_ref[...].astype(jnp.float32))

    edge_rows = jnp.zeros((WIN, kv.shape[1]), kv.dtype)

    @pl.when(me == 0)
    def _():
        kv[pl.ds(0, WIN)] = edge_rows

    @pl.when(me == ends)
    def _():
        kv[pl.ds(WIN + rows, WIN)] = edge_rows

    for load in loads:
        load.wait()
    forward(turn(0))
    project(turn(0))
    if chunks > 1:
        forward(turn(1))
    feed_forward(turn(0))

    @pl.loop(1, chunks)
    def _(step):
        project(turn(step))

        @pl.when(step + 1 < chunks)
        def _():
            forward(turn(step + 1))

    @pl.loop(1, chunks)
    def _(step):
        feed_forward(turn(step))

    @pl.when(me > 0)
    def _():
        for chunk in to_right:
            kv_copy(chunk, 1).wait_recv()

    @pl.when(me < ends)
    def _():
        for chunk in to_left:
            kv_copy(chunk, 0).wait_recv()

    def scatter_sub(chunk, k, m):
        return remote(
            parts.at[chunk, m * n_sub + sub_at(k)], in1.at[chunk, k - 1, m],
            r1_send.at[chunk, k - 1, m], r1_recv.at[chunk, k - 1, m], sub=sub_at(k),
        )

    def scatter_mp(chunk, j):
        return remote(
            out2.at[chunk, j - 1], in2.at[chunk, j - 1],
            r2_send.at[chunk, j - 1], r2_recv.at[chunk, j - 1], mp=mp_at(j),
        )

    pieces = (BLOCK + 2 * WIN) // BLOCK
    row = lax.broadcasted_iota(jnp.int32, (BLOCK, BLOCK), 0)
    lane = lax.broadcasted_iota(jnp.int32, (BLOCK, BLOCK), 1)
    front = lax.broadcasted_iota(jnp.int32, (BLOCK, 2 * HD), 1) < HD

    def attend(chunk):
        here = at_rows(chunk)

        def score(head):
            wide = slice(head * 2 * HD, (head + 1) * 2 * HD)
            query = queries[here, wide]
            scored, windows = [], []
            for piece in range(pieces):
                at = pl.multiple_of(chunk * BLOCK + piece * BLOCK, BLOCK)
                window = kv[pl.ds(at, BLOCK), wide]
                windows.append(jnp.where(front, jnp.bfloat16(1), window))
                part = lax.dot_general(
                    query, window, (((1,), (1,)), ((), ())), preferred_element_type=jnp.float32
                )
                if piece * BLOCK != WIN:
                    spot = me * rows + at - WIN
                    inside = (spot >= 0) & (spot < (ends + 1) * rows)
                    part = part + jnp.where(inside, 0.0, -1e30)
                if piece == 0:
                    part = jnp.where(lane >= row, part, -1e30)
                if piece == pieces - 1:
                    part = jnp.where(lane <= row, part, -1e30)
                scored.append(part)
            return jnp.concatenate(scored, axis=1), jnp.concatenate(windows, axis=0)

        later, outs = score(0), []
        for head in range(heads):
            (scores, window), later = later, score(head + 1) if head + 1 < heads else None
            peak = jnp.max(scores, axis=-1, keepdims=True)
            probs = jnp.exp(scores - peak).astype(jnp.bfloat16)
            mixed = jnp.dot(probs, window, preferred_element_type=jnp.float32)
            rolled = pltpu.roll(mixed, HD, 1)
            outs.append(rolled / mixed if head % 2 == 0 else mixed / rolled)
        pairs = [jnp.where(front, outs[i], outs[i + 1]) for i in range(0, heads, 2)]
        attended = jnp.concatenate(pairs, axis=1).astype(jnp.bfloat16)
        out = jnp.dot(attended, w_out[...], preferred_element_type=jnp.float32) + mlp[here, :]
        out = out.astype(jnp.bfloat16)
        for t in range(blocks):
            parts[chunk, t] = out[:, t * columns : (t + 1) * columns]
        for k in range(1, n_sub):
            for m in range(n_mp):
                scatter_sub(chunk, k, m).start()

    def chip_sum(chunk, m):
        total = parts[chunk, m * n_sub + sub].astype(jnp.float32)
        for k in range(1, n_sub):
            total += in1[chunk, k - 1, m].astype(jnp.float32)
        return total

    def pass_on(chunk):
        for k in range(1, n_sub):
            for m in range(n_mp):
                scatter_sub(chunk, k, m).wait_recv()
        for j in range(1, n_mp):
            out2[chunk, j - 1] = chip_sum(chunk, mp_at(j)).astype(jnp.bfloat16)
            scatter_mp(chunk, j).start()

    @pl.loop(0, chunks)
    def _(chunk):
        attend(chunk)

        @pl.when(chunk > 0)
        def _():
            pass_on(chunk - 1)

    pass_on(chunks - 1)

    @pl.loop(0, chunks)
    def _(chunk):
        here = at_rows(chunk)
        total = chip_sum(chunk, mp)
        for j in range(1, n_mp):
            scatter_mp(chunk, j).wait_recv()
            total += in2[chunk, j - 1].astype(jnp.float32)
        hidden_ref[here, :] = (full[own, here].astype(jnp.float32) + total).astype(jnp.bfloat16)

    finish_decoder = edge_messages(
        DSIDE, dec_src_ref, dec_weight_ref, hidden_ref, dec_sent, dec_messages, d_send, d_recv
    )
    wider = 2 * BLOCK

    @pl.loop(0, result_ref.shape[0] // wider)
    def _(step):
        first = pl.multiple_of(step * wider, wider)
        here = pl.ds(first, wider)
        total = scatter_group(dec_dst_ref[...], dec_messages[...], wider, first)
        total = grid_ref[here, :].astype(jnp.float32) + total
        live = lax.broadcasted_iota(jnp.int32, total.shape, 0) + first < count_ref[0]
        result_ref[here, :] = jnp.where(live, total, 0.0).astype(jnp.bfloat16)

    finish_edges()
    finish_decoder()

    @pl.loop(0, chunks)
    def _(chunk):
        for j in range(1, n_mp):
            gather_mp(chunk, j, own).wait_send()
            scatter_mp(chunk, j).wait_send()
        for k in range(1, n_sub):
            for j in range(n_mp):
                gather_sub(chunk, k, j, own).wait_send()
                scatter_sub(chunk, k, j).wait_send()

    @pl.when(me > 0)
    def _():
        for chunk in to_left:
            kv_copy(chunk, 0).wait_send()

    @pl.when(me < ends)
    def _():
        for chunk in to_right:
            kv_copy(chunk, 1).wait_send()


def layer(
    count, src, weight, dst, dec_src, dec_weight, dec_dst,
    grid, embed, gain, up_exp, down_exp, w_qkv, w_up, w_down, w_out,
):
    rows, columns = embed.shape
    n_mp, n_sub = lax.axis_size("mp"), lax.axis_size("sub")
    blocks, chunks = n_mp * n_sub, rows // BLOCK
    wide = w_qkv.shape[1] // (3 * HD) * 2 * HD
    half = lambda *shape: pltpu.VMEM(shape, jnp.bfloat16)
    full = lambda *shape: pltpu.VMEM(shape, jnp.float32)
    return pl.pallas_call(
        layer_kernel,
        out_shape=(
            jax.ShapeDtypeStruct((rows, columns), jnp.bfloat16),
            jax.ShapeDtypeStruct(grid.shape, jnp.bfloat16),
        ),
        in_specs=[pl.BlockSpec(memory_space=pltpu.SMEM)] + [VM] * 11
        + [pl.BlockSpec(memory_space=pl.ANY)] * 4,
        out_specs=(VM, VM),
        scratch_shapes=[
            half(2 * ESIDE * TILE, columns), half(src.size, columns),
            half(2 * DSIDE * TILE, columns), half(dec_src.size, columns),
            half(blocks, rows, columns), half(rows, w_qkv.shape[0]),
            half(rows, wide), half(rows + 2 * WIN, wide), full(rows, w_down.shape[1]),
            half(chunks, blocks, BLOCK, columns), half(chunks, n_sub - 1, n_mp, BLOCK, columns),
            half(chunks, n_mp - 1, BLOCK, columns), half(chunks, n_mp - 1, BLOCK, columns),
            half(*w_qkv.shape), half(*w_up.shape), half(*w_down.shape), half(*w_out.shape),
            DMA((4,)), DMA((2,)), DMA((2,)), DMA((2,)), DMA((2,)),
            DMA((n_mp - 1, chunks)), DMA((n_mp - 1, chunks)),
            DMA((n_sub - 1, n_mp, chunks)), DMA((n_sub - 1, n_mp, chunks)),
            DMA((2, chunks)), DMA((2, chunks)),
            DMA((chunks, n_sub - 1, n_mp)), DMA((chunks, n_sub - 1, n_mp)),
            DMA((chunks, n_mp - 1)), DMA((chunks, n_mp - 1)),
        ],
        compiler_params=pltpu.CompilerParams(
            vmem_limit_bytes=LIMIT, collective_id=0, has_side_effects=True
        ),
        name="encode_layer_decode",
    )(
        count, src, weight, dst, dec_src, dec_weight, dec_dst,
        grid, embed, gain, up_exp, down_exp, w_qkv, w_up, w_down, w_out,
    )


def hand_on_kernel(*refs):
    count = (len(refs) - 1) // 2
    sems = refs[-1]
    copies = []
    for i in range(count):
        half = refs[i].shape[0] // 2
        for j in range(2):
            here = pl.ds(j * half, half)
            copies.append(
                pltpu.make_async_copy(refs[i].at[here], refs[count + i].at[here], sems.at[2 * i + j])
            )
    for copy in copies:
        copy.start()
    for copy in copies:
        copy.wait()


def hand_on(*arrays):
    places = [pl.BlockSpec(memory_space=pl.ANY)] * len(arrays)
    return pl.pallas_call(
        hand_on_kernel,
        out_shape=tuple(jax.ShapeDtypeStruct(array.shape, array.dtype) for array in arrays),
        in_specs=places,
        out_specs=tuple(places),
        scratch_shapes=[DMA((2 * len(arrays),))],
        compiler_params=pltpu.CompilerParams(vmem_limit_bytes=LIMIT),
        name="hand_on",
    )(*arrays)


def shards(
    grid_latent, grid_count, hidden_embed, enc_src_rows, enc_dst_rows, enc_weight,
    dec_src_rows, dec_dst_rows, dec_weight, norm_gain, w_qkv, w_out, w_up, up_exp, w_down, down_exp,
):
    hidden_out, grid_out = layer(
        grid_count, enc_src_rows[0], enc_weight[0], enc_dst_rows[0],
        dec_src_rows[0], dec_weight[0], dec_dst_rows[0], grid_latent, hidden_embed,
        norm_gain[None, :], up_exp[None, :], down_exp[None, :], w_qkv, w_up, w_down, w_out,
    )
    return hand_on(hidden_out, grid_out)


def solution(mesh):
    rows = P(("ens", "seq"), ("mp", "sub"))
    tiles = P(("ens", "seq"), None, None)
    across, down = P(None, ("mp", "sub")), P(("mp", "sub"), None)
    placed = (
        rows, P(("ens", "seq")), rows, tiles, tiles, tiles, tiles, tiles, tiles,
        P(), across, down, across, P(("mp", "sub")), down, P(),
    )
    return jax.shard_map(shards, mesh=mesh, in_specs=placed, out_specs=(rows, rows), check_vma=False)
```

```python
import functools

import jax
import jax.numpy as jnp
from jax import lax
from jax.experimental import pallas as pl
from jax.experimental.pallas import tpu as pltpu
from jax.sharding import PartitionSpec as P

HD = 64
WIN = 512
TILE = 128
ESIDE = 4
DSIDE = 4
GROUP = 8
BLOCK = 256
LIMIT = 60 * 1024 * 1024
VM = pl.BlockSpec(memory_space=pltpu.VMEM)
DMA = pltpu.SemaphoreType.DMA
MESH = pl.DeviceIdType.MESH


def turned(row):
    return jnp.broadcast_to(row, (TILE, TILE)).T


def gather_group(src, weight, table, first=0):
    rows, columns = table.shape
    lane = lax.broadcasted_iota(jnp.int32, (TILE, rows), 1).astype(jnp.int16)
    picks, scales = [], []
    for tile in range(src.shape[0]):
        col = turned(src[tile : tile + 1] - first).astype(jnp.int16)
        col = jnp.concatenate([col] * (rows // TILE), axis=1)
        picks.append(jnp.where(lane == col, jnp.bfloat16(1), jnp.bfloat16(0)))
        scale = turned(weight[tile : tile + 1])
        scales.append(jnp.concatenate([scale] * (columns // TILE), axis=1))
    picked = jnp.dot(jnp.concatenate(picks, axis=0), table, preferred_element_type=jnp.float32)
    return (picked * jnp.concatenate(scales, axis=0)).astype(jnp.bfloat16)


def scatter_group(dst, messages, rows, first=0):
    line = lax.broadcasted_iota(jnp.int32, (rows, TILE), 0).astype(jnp.int16)
    spots = []
    for tile in range(dst.shape[0]):
        row = jnp.broadcast_to(dst[tile : tile + 1] - first, (16, TILE)).astype(jnp.int16)
        row = jnp.concatenate([row] * (rows // 16), axis=0)
        spots.append(jnp.where(line == row, jnp.bfloat16(1), jnp.bfloat16(0)))
    return jnp.dot(jnp.concatenate(spots, axis=1), messages, preferred_element_type=jnp.float32)


def remote(src, dst, send, recv, **where):
    return pltpu.make_async_remote_copy(
        src_ref=src, dst_ref=dst, send_sem=send, recv_sem=recv, device_id=where, device_id_type=MESH
    )


def greet(peers):
    me, ends = lax.axis_index("seq"), lax.axis_size("seq") - 1
    barrier = pltpu.get_barrier_semaphore()
    for peer in peers:
        pl.semaphore_signal(barrier, inc=1, device_id=peer, device_id_type=MESH)

    @pl.when(me > 0)
    def _():
        pl.semaphore_signal(barrier, inc=1, device_id={"seq": me - 1}, device_id_type=MESH)

    @pl.when(me < ends)
    def _():
        pl.semaphore_signal(barrier, inc=1, device_id={"seq": me + 1}, device_id_type=MESH)

    near = jnp.where(me > 0, 1, 0) + jnp.where(me < ends, 1, 0)
    pl.semaphore_wait(barrier, near + len(peers))


def side_copies(side, sent, messages, send, recv):
    me = lax.axis_index("seq")
    head, tail = pl.ds(0, side * TILE), pl.ds(side * TILE, side * TILE)
    to_left = remote(sent.at[head], messages.at[tail], send.at[0], recv.at[0], seq=me - 1)
    to_right = remote(sent.at[tail], messages.at[head], send.at[1], recv.at[1], seq=me + 1)
    return to_left, to_right


def start_sides(copies):
    me, ends = lax.axis_index("seq"), lax.axis_size("seq") - 1

    @pl.when(me > 0)
    def _():
        copies[0].start()

    @pl.when(me < ends)
    def _():
        copies[1].start()


def wait_sides(side, copies, messages):
    me, ends = lax.axis_index("seq"), lax.axis_size("seq") - 1
    blank = jnp.zeros((side * TILE, messages.shape[1]), messages.dtype)

    @pl.when(me > 0)
    def _():
        copies[1].wait_recv()

    @pl.when(me == 0)
    def _():
        messages[pl.ds(0, side * TILE)] = blank

    @pl.when(me < ends)
    def _():
        copies[0].wait_recv()

    @pl.when(me == ends)
    def _():
        messages[pl.ds(side * TILE, side * TILE)] = blank


def finish_sides(copies):
    me, ends = lax.axis_index("seq"), lax.axis_size("seq") - 1

    @pl.when(me > 0)
    def _():
        copies[0].wait_send()

    @pl.when(me < ends)
    def _():
        copies[1].wait_send()


def side_messages(side, src_ref, weight_ref, table, sent, first=0, add=False):
    found = gather_group(src_ref[: 2 * side], weight_ref[: 2 * side], table, first)
    sent[...] = sent[...] + found if add else found


def local_messages(side, src_ref, weight_ref, table_ref, messages, first=0, add=False):
    @pl.loop(2 * side // GROUP, src_ref.shape[0] // GROUP)
    def _(step):
        here = pl.ds(pl.multiple_of(step * GROUP, GROUP), GROUP)
        spots = pl.ds(pl.multiple_of(step * GROUP * TILE, GROUP * TILE), GROUP * TILE)
        found = gather_group(src_ref[here, :], weight_ref[here, :], table_ref[...], first)
        messages[spots, :] = messages[spots, :] + found if add else found


def local_sums(side, dst_ref, messages, sums, block):
    @pl.loop(0, sums.shape[0] // block)
    def _(step):
        first = pl.multiple_of(step * block, block)
        sums[pl.ds(first, block), :] = scatter_group(
            dst_ref[2 * side :], messages[2 * side * TILE :], block, first
        )


def arrived_sums(side, dst_ref, messages, block, first):
    return scatter_group(dst_ref[: 2 * side], messages[: 2 * side * TILE], block, first)


def layer_kernel(
    count_ref, src_ref, weight_ref, dst_ref, dec_src_ref, dec_weight_ref, dec_dst_ref,
    grid_ref, embed_ref, gain_ref, up_exp_ref, down_exp_ref,
    qkv_hbm, up_hbm, down_hbm, out_hbm, hidden_ref, result_ref,
    sums, sent, messages, dec_sent, dec_messages, full, normed, queries, kv, mlp, parts, in1, out2, in2,
    w_qkv, w_up, w_down, w_out,
    w_sem, z_send, z_recv, d_send, d_recv, ax_send, ax_recv, as_send, as_recv, kv_send, kv_recv,
    r1_send, r1_recv, r2_send, r2_recv,
):
    me, ends = lax.axis_index("seq"), lax.axis_size("seq") - 1
    mp, n_mp = lax.axis_index("mp"), lax.axis_size("mp")
    sub, n_sub = lax.axis_index("sub"), lax.axis_size("sub")
    rows, columns = embed_ref.shape
    blocks = n_mp * n_sub
    chunks = rows // BLOCK
    heads = queries.shape[1] // (2 * HD)
    own = mp * n_sub + sub

    loads = [
        pltpu.make_async_copy(src, dst, w_sem.at[i])
        for i, (src, dst) in enumerate(
            ((qkv_hbm, w_qkv), (up_hbm, w_up), (down_hbm, w_down), (out_hbm, w_out))
        )
    ]
    for load in loads:
        load.start()

    mp_at = lambda j: lax.rem(mp + j, n_mp)
    sub_at = lambda k: lax.rem(sub + k, n_sub)
    peers = [{"mp": mp_at(j)} for j in range(1, n_mp)] + [{"sub": sub_at(k)} for k in range(1, n_sub)]

    def at_rows(chunk):
        return pl.ds(pl.multiple_of(chunk * BLOCK, BLOCK), BLOCK)

    def gather_mp(chunk, j, owner):
        piece = full.at[owner, at_rows(chunk)]
        return remote(piece, piece, ax_send.at[j - 1, chunk], ax_recv.at[j - 1, chunk], mp=mp_at(j))

    def gather_sub(chunk, k, j, owner):
        piece = full.at[owner, at_rows(chunk)]
        return remote(
            piece, piece, as_send.at[k - 1, j, chunk], as_recv.at[k - 1, j, chunk], sub=sub_at(k)
        )

    from_mp = lambda j: lax.rem(mp + n_mp - j, n_mp)
    from_sub = lambda k: lax.rem(sub + n_sub - k, n_sub)

    encoder_copies = side_copies(ESIDE, sent, messages, z_send, z_recv)
    side_messages(ESIDE, src_ref, weight_ref, grid_ref[...], sent)
    greet(peers)
    start_sides(encoder_copies)
    local_messages(ESIDE, src_ref, weight_ref, grid_ref, messages)
    local_sums(ESIDE, dst_ref, messages, sums.at[pl.ds(0, rows)], 2 * BLOCK)
    wait_sides(ESIDE, encoder_copies, messages)

    def turn(step):
        return step % 2 * (chunks // 2) + step // 2 if chunks % 2 == 0 else step

    @pl.loop(0, chunks)
    def _(step):
        chunk = turn(step)
        here = at_rows(chunk)
        total = sums[here, :] + arrived_sums(ESIDE, dst_ref, messages, BLOCK, chunk * BLOCK)
        latent = embed_ref[here, :].astype(jnp.float32) + total
        full[own, here] = latent.astype(jnp.bfloat16)
        for j in range(1, n_mp):
            gather_mp(chunk, j, own).start()
        for k in range(1, n_sub):
            gather_sub(chunk, k, 0, own).start()

    def forward(chunk):
        for j in range(1, n_mp):
            owner = from_mp(j) * n_sub + sub
            gather_mp(chunk, j, owner).wait_recv()
            for k in range(1, n_sub):
                gather_sub(chunk, k, j, owner).start()

    def kv_copy(chunk, way):
        src = kv.at[pl.ds(pl.multiple_of(WIN + chunk * BLOCK, BLOCK), BLOCK)]
        shift = WIN + rows if way == 0 else WIN - rows
        dst = kv.at[pl.ds(pl.multiple_of(shift + chunk * BLOCK, BLOCK), BLOCK)]
        to = me - 1 if way == 0 else me + 1
        return remote(src, dst, kv_send.at[way, chunk], kv_recv.at[way, chunk], seq=to)

    to_left = range(WIN // BLOCK)
    to_right = range((rows - WIN) // BLOCK, chunks)

    def project(chunk):
        here = at_rows(chunk)
        for k in range(1, n_sub):
            for j in range(n_mp):
                owner = (from_mp(j) if j else mp) * n_sub + from_sub(k)
                gather_sub(chunk, k, j, owner).wait_recv()
        values = jnp.concatenate([full[t, here] for t in range(blocks)], axis=1).astype(jnp.float32)
        centered = values - jnp.mean(values, axis=-1, keepdims=True)
        row_var = jnp.mean(centered * centered, axis=-1, keepdims=True)
        rows_normed = (centered * lax.rsqrt(row_var + 1e-05) * gain_ref[...]).astype(jnp.bfloat16)
        normed[here, :] = rows_normed
        qkv = jnp.dot(rows_normed, w_qkv[...], preferred_element_type=jnp.float32)
        qkv = qkv.astype(jnp.bfloat16)
        blank = jnp.zeros((BLOCK, HD), jnp.bfloat16)
        inner = pl.ds(pl.multiple_of(WIN + chunk * BLOCK, BLOCK), BLOCK)
        for head in range(heads):
            at = head * 3 * HD
            wide = slice(head * 2 * HD, (head + 1) * 2 * HD)
            query = qkv[:, at : at + HD] * HD ** (-0.5)
            queries[here, wide] = jnp.concatenate([query, blank], axis=1)
            kv[inner, wide] = qkv[:, at + HD : at + 3 * HD]

        @pl.when((me > 0) & (chunk < to_left.stop))
        def _():
            kv_copy(chunk, 0).start()

        @pl.when((me < ends) & (chunk >= to_right.start))
        def _():
            kv_copy(chunk, 1).start()

    def feed_forward(chunk):
        here = at_rows(chunk)
        rows_normed = normed[here, :]
        units = w_up.shape[1]
        width = min(256, units)

        def rise(at):
            return jnp.dot(
                rows_normed, w_up[:, at : at + width], preferred_element_type=jnp.float32
            )

        later, pieces = rise(0), []
        for at in range(0, units, width):
            up, later = later, rise(at + width) if at + width < units else None
            up = up * jnp.exp2(up_exp_ref[:, at : at + width].astype(jnp.float32))
            pieces.append((0.5 * up * (1.0 + lax.erf(up * 0.5**0.5))).astype(jnp.bfloat16))
        active = jnp.concatenate(pieces, axis=1)
        down = jnp.dot(active, w_down[...], preferred_element_type=jnp.float32)
        mlp[here, :] = down * jnp.exp2(down_exp_ref[...].astype(jnp.float32))

    edge_rows = jnp.zeros((WIN, kv.shape[1]), kv.dtype)

    @pl.when(me == 0)
    def _():
        kv[pl.ds(0, WIN)] = edge_rows

    @pl.when(me == ends)
    def _():
        kv[pl.ds(WIN + rows, WIN)] = edge_rows

    for load in loads:
        load.wait()
    forward(turn(0))
    project(turn(0))
    if chunks > 1:
        forward(turn(1))
    feed_forward(turn(0))

    @pl.loop(1, chunks)
    def _(step):
        project(turn(step))

        @pl.when(step + 1 < chunks)
        def _():
            forward(turn(step + 1))

    @pl.loop(1, chunks)
    def _(step):
        feed_forward(turn(step))

    @pl.when(me > 0)
    def _():
        for chunk in to_right:
            kv_copy(chunk, 1).wait_recv()

    @pl.when(me < ends)
    def _():
        for chunk in to_left:
            kv_copy(chunk, 0).wait_recv()

    def scatter_sub(chunk, k, m):
        return remote(
            parts.at[chunk, m * n_sub + sub_at(k)], in1.at[chunk, k - 1, m],
            r1_send.at[chunk, k - 1, m], r1_recv.at[chunk, k - 1, m], sub=sub_at(k),
        )

    def scatter_mp(chunk, j):
        return remote(
            out2.at[chunk, j - 1], in2.at[chunk, j - 1],
            r2_send.at[chunk, j - 1], r2_recv.at[chunk, j - 1], mp=mp_at(j),
        )

    pieces = (BLOCK + 2 * WIN) // BLOCK
    row = lax.broadcasted_iota(jnp.int32, (BLOCK, BLOCK), 0)
    lane = lax.broadcasted_iota(jnp.int32, (BLOCK, BLOCK), 1)
    front = lax.broadcasted_iota(jnp.int32, (BLOCK, 2 * HD), 1) < HD

    def attend(chunk):
        here = at_rows(chunk)

        def score(head):
            wide = slice(head * 2 * HD, (head + 1) * 2 * HD)
            query = queries[here, wide]
            scored, windows = [], []
            for piece in range(pieces):
                at = pl.multiple_of(chunk * BLOCK + piece * BLOCK, BLOCK)
                window = kv[pl.ds(at, BLOCK), wide]
                windows.append(jnp.where(front, jnp.bfloat16(1), window))
                part = lax.dot_general(
                    query, window, (((1,), (1,)), ((), ())), preferred_element_type=jnp.float32
                )
                if piece * BLOCK != WIN:
                    spot = me * rows + at - WIN
                    inside = (spot >= 0) & (spot < (ends + 1) * rows)
                    part = part + jnp.where(inside, 0.0, -1e30)
                if piece == 0:
                    part = jnp.where(lane >= row, part, -1e30)
                if piece == pieces - 1:
                    part = jnp.where(lane <= row, part, -1e30)
                scored.append(part)
            return jnp.concatenate(scored, axis=1), jnp.concatenate(windows, axis=0)

        later, outs = score(0), []
        for head in range(heads):
            (scores, window), later = later, score(head + 1) if head + 1 < heads else None
            peak = jnp.max(scores, axis=-1, keepdims=True)
            probs = jnp.exp(scores - peak).astype(jnp.bfloat16)
            mixed = jnp.dot(probs, window, preferred_element_type=jnp.float32)
            rolled = pltpu.roll(mixed, HD, 1)
            outs.append(rolled / mixed if head % 2 == 0 else mixed / rolled)
        pairs = [jnp.where(front, outs[i], outs[i + 1]) for i in range(0, heads, 2)]
        attended = jnp.concatenate(pairs, axis=1).astype(jnp.bfloat16)
        out = jnp.dot(attended, w_out[...], preferred_element_type=jnp.float32) + mlp[here, :]
        out = out.astype(jnp.bfloat16)
        for t in range(blocks):
            parts[chunk, t] = out[:, t * columns : (t + 1) * columns]
        for k in range(1, n_sub):
            for m in range(n_mp):
                scatter_sub(chunk, k, m).start()

    def chip_sum(chunk, m):
        total = parts[chunk, m * n_sub + sub].astype(jnp.float32)
        for k in range(1, n_sub):
            total += in1[chunk, k - 1, m].astype(jnp.float32)
        return total

    def pass_on(chunk):
        for k in range(1, n_sub):
            for m in range(n_mp):
                scatter_sub(chunk, k, m).wait_recv()
        for j in range(1, n_mp):
            out2[chunk, j - 1] = chip_sum(chunk, mp_at(j)).astype(jnp.bfloat16)
            scatter_mp(chunk, j).start()

    @pl.loop(0, chunks)
    def _(chunk):
        attend(chunk)

        @pl.when(chunk > 0)
        def _():
            pass_on(chunk - 1)

    pass_on(chunks - 1)

    def finish_rows(chunk):
        here = at_rows(chunk)
        total = chip_sum(chunk, mp)
        for j in range(1, n_mp):
            scatter_mp(chunk, j).wait_recv()
            total += in2[chunk, j - 1].astype(jnp.float32)
        hidden_ref[here, :] = (full[own, here].astype(jnp.float32) + total).astype(jnp.bfloat16)

    early = rows - BLOCK
    if early:
        @pl.loop(0, chunks - 1)
        def _(chunk):
            finish_rows(chunk)

        first_rows = hidden_ref.at[pl.ds(0, early)]
        side_messages(DSIDE, dec_src_ref, dec_weight_ref, first_rows[...], dec_sent)
        local_messages(DSIDE, dec_src_ref, dec_weight_ref, first_rows, dec_messages)
    finish_rows(chunks - 1)
    last_rows = hidden_ref.at[pl.ds(early, BLOCK)]
    more = early > 0
    decoder_copies = side_copies(DSIDE, dec_sent, dec_messages, d_send, d_recv)
    side_messages(DSIDE, dec_src_ref, dec_weight_ref, last_rows[...], dec_sent, early, more)
    start_sides(decoder_copies)
    local_messages(DSIDE, dec_src_ref, dec_weight_ref, last_rows, dec_messages, early, more)
    wider = 2 * BLOCK
    local_sums(DSIDE, dec_dst_ref, dec_messages, sums, wider)
    wait_sides(DSIDE, decoder_copies, dec_messages)

    @pl.loop(0, result_ref.shape[0] // wider)
    def _(step):
        first = pl.multiple_of(step * wider, wider)
        here = pl.ds(first, wider)
        total = sums[here, :] + arrived_sums(DSIDE, dec_dst_ref, dec_messages, wider, first)
        total = grid_ref[here, :].astype(jnp.float32) + total
        live = lax.broadcasted_iota(jnp.int32, total.shape, 0) + first < count_ref[0]
        result_ref[here, :] = jnp.where(live, total, 0.0).astype(jnp.bfloat16)

    finish_sides(encoder_copies)
    finish_sides(decoder_copies)

    @pl.loop(0, chunks)
    def _(chunk):
        for j in range(1, n_mp):
            gather_mp(chunk, j, own).wait_send()
            scatter_mp(chunk, j).wait_send()
        for k in range(1, n_sub):
            for j in range(n_mp):
                gather_sub(chunk, k, j, own).wait_send()
                scatter_sub(chunk, k, j).wait_send()

    @pl.when(me > 0)
    def _():
        for chunk in to_left:
            kv_copy(chunk, 0).wait_send()

    @pl.when(me < ends)
    def _():
        for chunk in to_right:
            kv_copy(chunk, 1).wait_send()


def layer(
    count, src, weight, dst, dec_src, dec_weight, dec_dst,
    grid, embed, gain, up_exp, down_exp, w_qkv, w_up, w_down, w_out,
):
    rows, columns = embed.shape
    n_mp, n_sub = lax.axis_size("mp"), lax.axis_size("sub")
    blocks, chunks = n_mp * n_sub, rows // BLOCK
    wide = w_qkv.shape[1] // (3 * HD) * 2 * HD
    half = lambda *shape: pltpu.VMEM(shape, jnp.bfloat16)
    full = lambda *shape: pltpu.VMEM(shape, jnp.float32)
    return pl.pallas_call(
        layer_kernel,
        out_shape=(
            jax.ShapeDtypeStruct((rows, columns), jnp.bfloat16),
            jax.ShapeDtypeStruct(grid.shape, jnp.bfloat16),
        ),
        in_specs=[pl.BlockSpec(memory_space=pltpu.SMEM)] + [VM] * 11
        + [pl.BlockSpec(memory_space=pl.ANY)] * 4,
        out_specs=(VM, VM),
        scratch_shapes=[
            full(max(rows, grid.shape[0]), columns),
            half(2 * ESIDE * TILE, columns), half(src.size, columns),
            half(2 * DSIDE * TILE, columns), half(dec_src.size, columns),
            half(blocks, rows, columns), half(rows, w_qkv.shape[0]),
            half(rows, wide), half(rows + 2 * WIN, wide), full(rows, w_down.shape[1]),
            half(chunks, blocks, BLOCK, columns), half(chunks, n_sub - 1, n_mp, BLOCK, columns),
            half(chunks, n_mp - 1, BLOCK, columns), half(chunks, n_mp - 1, BLOCK, columns),
            half(*w_qkv.shape), half(*w_up.shape), half(*w_down.shape), half(*w_out.shape),
            DMA((4,)), DMA((2,)), DMA((2,)), DMA((2,)), DMA((2,)),
            DMA((n_mp - 1, chunks)), DMA((n_mp - 1, chunks)),
            DMA((n_sub - 1, n_mp, chunks)), DMA((n_sub - 1, n_mp, chunks)),
            DMA((2, chunks)), DMA((2, chunks)),
            DMA((chunks, n_sub - 1, n_mp)), DMA((chunks, n_sub - 1, n_mp)),
            DMA((chunks, n_mp - 1)), DMA((chunks, n_mp - 1)),
        ],
        compiler_params=pltpu.CompilerParams(
            vmem_limit_bytes=LIMIT, collective_id=0, has_side_effects=True
        ),
        name="encode_layer_decode",
    )(
        count, src, weight, dst, dec_src, dec_weight, dec_dst,
        grid, embed, gain, up_exp, down_exp, w_qkv, w_up, w_down, w_out,
    )


def hand_on_kernel(*refs):
    count = len(refs) // 2
    for source, target in zip(refs[:count], refs[count:]):
        target[...] = source[...]


def hand_on(*arrays):
    steps = 4
    places = [
        pl.BlockSpec((array.shape[0] // steps, array.shape[1]), lambda i: (i, 0)) for array in arrays
    ]
    return pl.pallas_call(
        hand_on_kernel,
        grid=(steps,),
        out_shape=tuple(jax.ShapeDtypeStruct(array.shape, array.dtype) for array in arrays),
        in_specs=places,
        out_specs=tuple(places),
        compiler_params=pltpu.CompilerParams(vmem_limit_bytes=LIMIT),
        name="hand_on",
    )(*arrays)


def shards(
    grid_latent, grid_count, hidden_embed, enc_src_rows, enc_dst_rows, enc_weight,
    dec_src_rows, dec_dst_rows, dec_weight, norm_gain, w_qkv, w_out, w_up, up_exp, w_down, down_exp,
):
    hidden_out, grid_out = layer(
        grid_count, enc_src_rows[0], enc_weight[0], enc_dst_rows[0],
        dec_src_rows[0], dec_weight[0], dec_dst_rows[0], grid_latent, hidden_embed,
        norm_gain[None, :], up_exp[None, :], down_exp[None, :], w_qkv, w_up, w_down, w_out,
    )
    return hand_on(hidden_out, grid_out)


def solution(mesh):
    rows = P(("ens", "seq"), ("mp", "sub"))
    tiles = P(("ens", "seq"), None, None)
    across, down = P(None, ("mp", "sub")), P(("mp", "sub"), None)
    placed = (
        rows, P(("ens", "seq")), rows, tiles, tiles, tiles, tiles, tiles, tiles,
        P(), across, down, across, P(("mp", "sub")), down, P(),
    )
    return jax.shard_map(shards, mesh=mesh, in_specs=placed, out_specs=(rows, rows), check_vma=False)
```

```python
import functools

import jax
import jax.numpy as jnp
from jax import lax
from jax.experimental import pallas as pl
from jax.experimental.pallas import tpu as pltpu
from jax.sharding import PartitionSpec as P

HD = 64
WIN = 512
TILE = 128
ESIDE = 4
DSIDE = 4
GROUP = 8
BLOCK = 256
LIMIT = 60 * 1024 * 1024
VM = pl.BlockSpec(memory_space=pltpu.VMEM)
DMA = pltpu.SemaphoreType.DMA
MESH = pl.DeviceIdType.MESH


def turned(src, weight):
    tiles = src.shape[0]
    blank = jnp.zeros((TILE - 2 * tiles, TILE), jnp.float32)
    both = jnp.concatenate([src.astype(jnp.float32), weight, blank], axis=0).T
    return both[:, :tiles].astype(jnp.int32), both[:, tiles : 2 * tiles]


def widened(columns, tile):
    return jnp.broadcast_to(columns[:, tile : tile + 1], (TILE, TILE))


def gather_group(src, weight, table, first=0):
    rows, columns = table.shape
    lane = lax.broadcasted_iota(jnp.int32, (TILE, rows), 1).astype(jnp.int16)
    picks, scales = [], []
    src, weight = turned(src - first, weight)
    for tile in range(src.shape[1]):
        col = widened(src, tile).astype(jnp.int16)
        col = jnp.concatenate([col] * (rows // TILE), axis=1)
        picks.append(jnp.where(lane == col, jnp.bfloat16(1), jnp.bfloat16(0)))
        scale = widened(weight, tile)
        scales.append(jnp.concatenate([scale] * (columns // TILE), axis=1))
    picked = jnp.dot(jnp.concatenate(picks, axis=0), table, preferred_element_type=jnp.float32)
    return (picked * jnp.concatenate(scales, axis=0)).astype(jnp.bfloat16)


def scatter_group(dst, messages, rows, first=0):
    line = lax.broadcasted_iota(jnp.int32, (rows, TILE), 0).astype(jnp.int16)
    spots = []
    for tile in range(dst.shape[0]):
        row = jnp.broadcast_to(dst[tile : tile + 1] - first, (16, TILE)).astype(jnp.int16)
        row = jnp.concatenate([row] * (rows // 16), axis=0)
        spots.append(jnp.where(line == row, jnp.bfloat16(1), jnp.bfloat16(0)))
    return jnp.dot(jnp.concatenate(spots, axis=1), messages, preferred_element_type=jnp.float32)


def remote(src, dst, send, recv, **where):
    return pltpu.make_async_remote_copy(
        src_ref=src, dst_ref=dst, send_sem=send, recv_sem=recv, device_id=where, device_id_type=MESH
    )


def greet(peers):
    me, ends = lax.axis_index("seq"), lax.axis_size("seq") - 1
    barrier = pltpu.get_barrier_semaphore()
    for peer in peers:
        pl.semaphore_signal(barrier, inc=1, device_id=peer, device_id_type=MESH)

    @pl.when(me > 0)
    def _():
        pl.semaphore_signal(barrier, inc=1, device_id={"seq": me - 1}, device_id_type=MESH)

    @pl.when(me < ends)
    def _():
        pl.semaphore_signal(barrier, inc=1, device_id={"seq": me + 1}, device_id_type=MESH)

    near = jnp.where(me > 0, 1, 0) + jnp.where(me < ends, 1, 0)
    pl.semaphore_wait(barrier, near + len(peers))


def side_copies(side, sent, messages, send, recv):
    me = lax.axis_index("seq")
    head, tail = pl.ds(0, side * TILE), pl.ds(side * TILE, side * TILE)
    to_left = remote(sent.at[head], messages.at[tail], send.at[0], recv.at[0], seq=me - 1)
    to_right = remote(sent.at[tail], messages.at[head], send.at[1], recv.at[1], seq=me + 1)
    return to_left, to_right


def start_sides(copies):
    me, ends = lax.axis_index("seq"), lax.axis_size("seq") - 1

    @pl.when(me > 0)
    def _():
        copies[0].start()

    @pl.when(me < ends)
    def _():
        copies[1].start()


def wait_sides(side, copies, messages):
    me, ends = lax.axis_index("seq"), lax.axis_size("seq") - 1
    blank = jnp.zeros((side * TILE, messages.shape[1]), messages.dtype)

    @pl.when(me > 0)
    def _():
        copies[1].wait_recv()

    @pl.when(me == 0)
    def _():
        messages[pl.ds(0, side * TILE)] = blank

    @pl.when(me < ends)
    def _():
        copies[0].wait_recv()

    @pl.when(me == ends)
    def _():
        messages[pl.ds(side * TILE, side * TILE)] = blank


def finish_sides(copies):
    me, ends = lax.axis_index("seq"), lax.axis_size("seq") - 1

    @pl.when(me > 0)
    def _():
        copies[0].wait_send()

    @pl.when(me < ends)
    def _():
        copies[1].wait_send()


def side_messages(side, src_ref, weight_ref, table, sent, first=0, add=False):
    found = gather_group(src_ref[: 2 * side], weight_ref[: 2 * side], table, first)
    sent[...] = sent[...] + found if add else found


def local_messages(side, src_ref, weight_ref, table_ref, messages, first=0, add=False):
    @pl.loop(2 * side // GROUP, src_ref.shape[0] // GROUP)
    def _(step):
        here = pl.ds(pl.multiple_of(step * GROUP, GROUP), GROUP)
        spots = pl.ds(pl.multiple_of(step * GROUP * TILE, GROUP * TILE), GROUP * TILE)
        found = gather_group(src_ref[here, :], weight_ref[here, :], table_ref[...], first)
        messages[spots, :] = messages[spots, :] + found if add else found


def local_sums(side, dst_ref, messages, sums, block):
    @pl.loop(0, sums.shape[0] // block)
    def _(step):
        first = pl.multiple_of(step * block, block)
        sums[pl.ds(first, block), :] = scatter_group(
            dst_ref[2 * side :], messages[2 * side * TILE :], block, first
        )


def arrived_sums(side, dst_ref, messages, block, first):
    return scatter_group(dst_ref[: 2 * side], messages[: 2 * side * TILE], block, first)


def layer_kernel(
    count_ref, src_ref, weight_ref, dst_ref, dec_src_ref, dec_weight_ref, dec_dst_ref,
    grid_ref, embed_ref, gain_ref, up_exp_ref, down_exp_ref,
    qkv_hbm, up_hbm, down_hbm, out_hbm, hidden_ref, result_ref,
    sums, sent, messages, dec_sent, dec_messages, full, normed, queries, kv, mlp, parts, in1, out2, in2,
    w_qkv, w_up, w_down, w_out,
    w_sem, z_send, z_recv, d_send, d_recv, ax_send, ax_recv, as_send, as_recv, kv_send, kv_recv,
    r1_send, r1_recv, r2_send, r2_recv,
):
    me, ends = lax.axis_index("seq"), lax.axis_size("seq") - 1
    mp, n_mp = lax.axis_index("mp"), lax.axis_size("mp")
    sub, n_sub = lax.axis_index("sub"), lax.axis_size("sub")
    rows, columns = embed_ref.shape
    blocks = n_mp * n_sub
    chunks = rows // BLOCK
    heads = queries.shape[1] // (2 * HD)
    own = mp * n_sub + sub

    loads = [
        pltpu.make_async_copy(src, dst, w_sem.at[i])
        for i, (src, dst) in enumerate(
            ((qkv_hbm, w_qkv), (up_hbm, w_up), (down_hbm, w_down), (out_hbm, w_out))
        )
    ]
    for load in loads:
        load.start()

    mp_at = lambda j: lax.rem(mp + j, n_mp)
    sub_at = lambda k: lax.rem(sub + k, n_sub)
    peers = [{"mp": mp_at(j)} for j in range(1, n_mp)] + [{"sub": sub_at(k)} for k in range(1, n_sub)]

    def at_rows(chunk):
        return pl.ds(pl.multiple_of(chunk * BLOCK, BLOCK), BLOCK)

    def gather_mp(chunk, j, owner):
        piece = full.at[owner, at_rows(chunk)]
        return remote(piece, piece, ax_send.at[j - 1, chunk], ax_recv.at[j - 1, chunk], mp=mp_at(j))

    def gather_sub(chunk, k, j, owner):
        piece = full.at[owner, at_rows(chunk)]
        return remote(
            piece, piece, as_send.at[k - 1, j, chunk], as_recv.at[k - 1, j, chunk], sub=sub_at(k)
        )

    from_mp = lambda j: lax.rem(mp + n_mp - j, n_mp)
    from_sub = lambda k: lax.rem(sub + n_sub - k, n_sub)

    encoder_copies = side_copies(ESIDE, sent, messages, z_send, z_recv)
    side_messages(ESIDE, src_ref, weight_ref, grid_ref[...], sent)
    greet(peers)
    start_sides(encoder_copies)
    local_messages(ESIDE, src_ref, weight_ref, grid_ref, messages)
    local_sums(ESIDE, dst_ref, messages, sums.at[pl.ds(0, rows)], 2 * BLOCK)
    wait_sides(ESIDE, encoder_copies, messages)

    def turn(step):
        return step % 2 * (chunks // 2) + step // 2 if chunks % 2 == 0 else step

    @pl.loop(0, chunks)
    def _(step):
        chunk = turn(step)
        here = at_rows(chunk)
        total = sums[here, :] + arrived_sums(ESIDE, dst_ref, messages, BLOCK, chunk * BLOCK)
        latent = embed_ref[here, :].astype(jnp.float32) + total
        full[own, here] = latent.astype(jnp.bfloat16)
        for j in range(1, n_mp):
            gather_mp(chunk, j, own).start()
        for k in range(1, n_sub):
            gather_sub(chunk, k, 0, own).start()

    def forward(chunk):
        for j in range(1, n_mp):
            owner = from_mp(j) * n_sub + sub
            gather_mp(chunk, j, owner).wait_recv()
            for k in range(1, n_sub):
                gather_sub(chunk, k, j, owner).start()

    def kv_copy(chunk, way):
        src = kv.at[pl.ds(pl.multiple_of(WIN + chunk * BLOCK, BLOCK), BLOCK)]
        shift = WIN + rows if way == 0 else WIN - rows
        dst = kv.at[pl.ds(pl.multiple_of(shift + chunk * BLOCK, BLOCK), BLOCK)]
        to = me - 1 if way == 0 else me + 1
        return remote(src, dst, kv_send.at[way, chunk], kv_recv.at[way, chunk], seq=to)

    to_left = range(WIN // BLOCK)
    to_right = range((rows - WIN) // BLOCK, chunks)

    def project(chunk):
        here = at_rows(chunk)
        for k in range(1, n_sub):
            for j in range(n_mp):
                owner = (from_mp(j) if j else mp) * n_sub + from_sub(k)
                gather_sub(chunk, k, j, owner).wait_recv()
        values = jnp.concatenate([full[t, here] for t in range(blocks)], axis=1).astype(jnp.float32)
        centered = values - jnp.mean(values, axis=-1, keepdims=True)
        row_var = jnp.mean(centered * centered, axis=-1, keepdims=True)
        rows_normed = (centered * lax.rsqrt(row_var + 1e-05) * gain_ref[...]).astype(jnp.bfloat16)
        normed[here, :] = rows_normed
        qkv = jnp.dot(rows_normed, w_qkv[...], preferred_element_type=jnp.float32)
        qkv = qkv.astype(jnp.bfloat16)
        blank = jnp.zeros((BLOCK, HD), jnp.bfloat16)
        inner = pl.ds(pl.multiple_of(WIN + chunk * BLOCK, BLOCK), BLOCK)
        for head in range(heads):
            at = head * 3 * HD
            wide = slice(head * 2 * HD, (head + 1) * 2 * HD)
            query = qkv[:, at : at + HD] * HD ** (-0.5)
            queries[here, wide] = jnp.concatenate([query, blank], axis=1)
            kv[inner, wide] = qkv[:, at + HD : at + 3 * HD]

        @pl.when((me > 0) & (chunk < to_left.stop))
        def _():
            kv_copy(chunk, 0).start()

        @pl.when((me < ends) & (chunk >= to_right.start))
        def _():
            kv_copy(chunk, 1).start()

    def feed_forward(chunk):
        here = at_rows(chunk)
        rows_normed = normed[here, :]
        units = w_up.shape[1]
        width = min(256, units)

        def rise(at):
            return jnp.dot(
                rows_normed, w_up[:, at : at + width], preferred_element_type=jnp.float32
            )

        later, pieces = rise(0), []
        for at in range(0, units, width):
            up, later = later, rise(at + width) if at + width < units else None
            up = up * jnp.exp2(up_exp_ref[:, at : at + width].astype(jnp.float32))
            pieces.append((0.5 * up * (1.0 + lax.erf(up * 0.5**0.5))).astype(jnp.bfloat16))
        active = jnp.concatenate(pieces, axis=1)
        down = jnp.dot(active, w_down[...], preferred_element_type=jnp.float32)
        mlp[here, :] = down * jnp.exp2(down_exp_ref[...].astype(jnp.float32))

    edge_rows = jnp.zeros((WIN, kv.shape[1]), kv.dtype)

    @pl.when(me == 0)
    def _():
        kv[pl.ds(0, WIN)] = edge_rows

    @pl.when(me == ends)
    def _():
        kv[pl.ds(WIN + rows, WIN)] = edge_rows

    for load in loads:
        load.wait()
    forward(turn(0))

    @pl.loop(0, chunks)
    def _(step):
        project(turn(step))

        @pl.when(step + 1 < chunks)
        def _():
            forward(turn(step + 1))

        @pl.when(step < chunks // 2)
        def _():
            feed_forward(turn(step))

    @pl.loop(chunks // 2, chunks)
    def _(step):
        feed_forward(turn(step))

    @pl.when(me > 0)
    def _():
        for chunk in to_right:
            kv_copy(chunk, 1).wait_recv()

    @pl.when(me < ends)
    def _():
        for chunk in to_left:
            kv_copy(chunk, 0).wait_recv()

    def scatter_sub(chunk, k, m):
        return remote(
            parts.at[chunk, m * n_sub + sub_at(k)], in1.at[chunk, k - 1, m],
            r1_send.at[chunk, k - 1, m], r1_recv.at[chunk, k - 1, m], sub=sub_at(k),
        )

    def scatter_mp(chunk, j):
        return remote(
            out2.at[chunk, j - 1], in2.at[chunk, j - 1],
            r2_send.at[chunk, j - 1], r2_recv.at[chunk, j - 1], mp=mp_at(j),
        )

    pieces = (BLOCK + 2 * WIN) // BLOCK
    row = lax.broadcasted_iota(jnp.int32, (BLOCK, BLOCK), 0)
    lane = lax.broadcasted_iota(jnp.int32, (BLOCK, BLOCK), 1)
    front = lax.broadcasted_iota(jnp.int32, (BLOCK, 2 * HD), 1) < HD

    def attend(chunk):
        here = at_rows(chunk)

        def score(head):
            wide = slice(head * 2 * HD, (head + 1) * 2 * HD)
            query = queries[here, wide]
            scored, windows = [], []
            for piece in range(pieces):
                at = pl.multiple_of(chunk * BLOCK + piece * BLOCK, BLOCK)
                window = kv[pl.ds(at, BLOCK), wide]
                windows.append(jnp.where(front, jnp.bfloat16(1), window))
                part = lax.dot_general(
                    query, window, (((1,), (1,)), ((), ())), preferred_element_type=jnp.float32
                )
                if piece * BLOCK != WIN:
                    spot = me * rows + at - WIN
                    inside = (spot >= 0) & (spot < (ends + 1) * rows)
                    part = part + jnp.where(inside, 0.0, -1e30)
                if piece == 0:
                    part = jnp.where(lane >= row, part, -1e30)
                if piece == pieces - 1:
                    part = jnp.where(lane <= row, part, -1e30)
                scored.append(part)
            return jnp.concatenate(scored, axis=1), jnp.concatenate(windows, axis=0)

        later, outs = score(0), []
        for head in range(heads):
            (scores, window), later = later, score(head + 1) if head + 1 < heads else None
            peak = jnp.max(scores, axis=-1, keepdims=True)
            probs = jnp.exp(scores - peak).astype(jnp.bfloat16)
            mixed = jnp.dot(probs, window, preferred_element_type=jnp.float32)
            rolled = pltpu.roll(mixed, HD, 1)
            outs.append(rolled / mixed if head % 2 == 0 else mixed / rolled)
        pairs = [jnp.where(front, outs[i], outs[i + 1]) for i in range(0, heads, 2)]
        attended = jnp.concatenate(pairs, axis=1).astype(jnp.bfloat16)
        out = jnp.dot(attended, w_out[...], preferred_element_type=jnp.float32) + mlp[here, :]
        out = out.astype(jnp.bfloat16)
        for t in range(blocks):
            parts[chunk, t] = out[:, t * columns : (t + 1) * columns]
        for k in range(1, n_sub):
            for m in range(n_mp):
                scatter_sub(chunk, k, m).start()

    def chip_sum(chunk, m):
        total = parts[chunk, m * n_sub + sub].astype(jnp.float32)
        for k in range(1, n_sub):
            total += in1[chunk, k - 1, m].astype(jnp.float32)
        return total

    def pass_on(chunk):
        for k in range(1, n_sub):
            for m in range(n_mp):
                scatter_sub(chunk, k, m).wait_recv()
        for j in range(1, n_mp):
            out2[chunk, j - 1] = chip_sum(chunk, mp_at(j)).astype(jnp.bfloat16)
            scatter_mp(chunk, j).start()

    @pl.loop(0, chunks)
    def _(chunk):
        attend(chunk)

        @pl.when(chunk > 0)
        def _():
            pass_on(chunk - 1)

    pass_on(chunks - 1)

    def finish_rows(chunk):
        here = at_rows(chunk)
        total = chip_sum(chunk, mp)
        for j in range(1, n_mp):
            scatter_mp(chunk, j).wait_recv()
            total += in2[chunk, j - 1].astype(jnp.float32)
        hidden_ref[here, :] = (full[own, here].astype(jnp.float32) + total).astype(jnp.bfloat16)

    early = rows - BLOCK
    if early:
        @pl.loop(0, chunks - 1)
        def _(chunk):
            finish_rows(chunk)

        first_rows = hidden_ref.at[pl.ds(0, early)]
        side_messages(DSIDE, dec_src_ref, dec_weight_ref, first_rows[...], dec_sent)
        local_messages(DSIDE, dec_src_ref, dec_weight_ref, first_rows, dec_messages)
    finish_rows(chunks - 1)
    last_rows = hidden_ref.at[pl.ds(early, BLOCK)]
    more = early > 0
    decoder_copies = side_copies(DSIDE, dec_sent, dec_messages, d_send, d_recv)
    side_messages(DSIDE, dec_src_ref, dec_weight_ref, last_rows[...], dec_sent, early, more)
    start_sides(decoder_copies)
    local_messages(DSIDE, dec_src_ref, dec_weight_ref, last_rows, dec_messages, early, more)
    wider = 2 * BLOCK
    local_sums(DSIDE, dec_dst_ref, dec_messages, sums, wider)
    wait_sides(DSIDE, decoder_copies, dec_messages)

    @pl.loop(0, result_ref.shape[0] // wider)
    def _(step):
        first = pl.multiple_of(step * wider, wider)
        here = pl.ds(first, wider)
        total = sums[here, :] + arrived_sums(DSIDE, dec_dst_ref, dec_messages, wider, first)
        total = grid_ref[here, :].astype(jnp.float32) + total
        live = lax.broadcasted_iota(jnp.int32, total.shape, 0) + first < count_ref[0]
        result_ref[here, :] = jnp.where(live, total, 0.0).astype(jnp.bfloat16)

    finish_sides(encoder_copies)
    finish_sides(decoder_copies)

    @pl.loop(0, chunks)
    def _(chunk):
        for j in range(1, n_mp):
            gather_mp(chunk, j, own).wait_send()
            scatter_mp(chunk, j).wait_send()
        for k in range(1, n_sub):
            for j in range(n_mp):
                gather_sub(chunk, k, j, own).wait_send()
                scatter_sub(chunk, k, j).wait_send()

    @pl.when(me > 0)
    def _():
        for chunk in to_left:
            kv_copy(chunk, 0).wait_send()

    @pl.when(me < ends)
    def _():
        for chunk in to_right:
            kv_copy(chunk, 1).wait_send()


def layer(
    count, src, weight, dst, dec_src, dec_weight, dec_dst,
    grid, embed, gain, up_exp, down_exp, w_qkv, w_up, w_down, w_out,
):
    rows, columns = embed.shape
    n_mp, n_sub = lax.axis_size("mp"), lax.axis_size("sub")
    blocks, chunks = n_mp * n_sub, rows // BLOCK
    wide = w_qkv.shape[1] // (3 * HD) * 2 * HD
    half = lambda *shape: pltpu.VMEM(shape, jnp.bfloat16)
    full = lambda *shape: pltpu.VMEM(shape, jnp.float32)
    return pl.pallas_call(
        layer_kernel,
        out_shape=(
            jax.ShapeDtypeStruct((rows, columns), jnp.bfloat16),
            jax.ShapeDtypeStruct(grid.shape, jnp.bfloat16),
        ),
        in_specs=[pl.BlockSpec(memory_space=pltpu.SMEM)] + [VM] * 11
        + [pl.BlockSpec(memory_space=pl.ANY)] * 4,
        out_specs=(VM, VM),
        scratch_shapes=[
            full(max(rows, grid.shape[0]), columns),
            half(2 * ESIDE * TILE, columns), half(src.size, columns),
            half(2 * DSIDE * TILE, columns), half(dec_src.size, columns),
            half(blocks, rows, columns), half(rows, w_qkv.shape[0]),
            half(rows, wide), half(rows + 2 * WIN, wide), full(rows, w_down.shape[1]),
            half(chunks, blocks, BLOCK, columns), half(chunks, n_sub - 1, n_mp, BLOCK, columns),
            half(chunks, n_mp - 1, BLOCK, columns), half(chunks, n_mp - 1, BLOCK, columns),
            half(*w_qkv.shape), half(*w_up.shape), half(*w_down.shape), half(*w_out.shape),
            DMA((4,)), DMA((2,)), DMA((2,)), DMA((2,)), DMA((2,)),
            DMA((n_mp - 1, chunks)), DMA((n_mp - 1, chunks)),
            DMA((n_sub - 1, n_mp, chunks)), DMA((n_sub - 1, n_mp, chunks)),
            DMA((2, chunks)), DMA((2, chunks)),
            DMA((chunks, n_sub - 1, n_mp)), DMA((chunks, n_sub - 1, n_mp)),
            DMA((chunks, n_mp - 1)), DMA((chunks, n_mp - 1)),
        ],
        compiler_params=pltpu.CompilerParams(
            vmem_limit_bytes=LIMIT, collective_id=0, has_side_effects=True
        ),
        name="encode_layer_decode",
    )(
        count, src, weight, dst, dec_src, dec_weight, dec_dst,
        grid, embed, gain, up_exp, down_exp, w_qkv, w_up, w_down, w_out,
    )


def hand_on_kernel(*refs):
    count = len(refs) // 2
    for source, target in zip(refs[:count], refs[count:]):
        target[...] = source[...]


def hand_on(*arrays):
    steps = 4
    places = [
        pl.BlockSpec((array.shape[0] // steps, array.shape[1]), lambda i: (i, 0)) for array in arrays
    ]
    return pl.pallas_call(
        hand_on_kernel,
        grid=(steps,),
        out_shape=tuple(jax.ShapeDtypeStruct(array.shape, array.dtype) for array in arrays),
        in_specs=places,
        out_specs=tuple(places),
        compiler_params=pltpu.CompilerParams(vmem_limit_bytes=LIMIT),
        name="hand_on",
    )(*arrays)


def shards(
    grid_latent, grid_count, hidden_embed, enc_src_rows, enc_dst_rows, enc_weight,
    dec_src_rows, dec_dst_rows, dec_weight, norm_gain, w_qkv, w_out, w_up, up_exp, w_down, down_exp,
):
    hidden_out, grid_out = layer(
        grid_count, enc_src_rows[0], enc_weight[0], enc_dst_rows[0],
        dec_src_rows[0], dec_weight[0], dec_dst_rows[0], grid_latent, hidden_embed,
        norm_gain[None, :], up_exp[None, :], down_exp[None, :], w_qkv, w_up, w_down, w_out,
    )
    return hand_on(hidden_out, grid_out)


def solution(mesh):
    rows = P(("ens", "seq"), ("mp", "sub"))
    tiles = P(("ens", "seq"), None, None)
    across, down = P(None, ("mp", "sub")), P(("mp", "sub"), None)
    placed = (
        rows, P(("ens", "seq")), rows, tiles, tiles, tiles, tiles, tiles, tiles,
        P(), across, down, across, P(("mp", "sub")), down, P(),
    )
    return jax.shard_map(shards, mesh=mesh, in_specs=placed, out_specs=(rows, rows), check_vma=False)
```
